32 devices in a mesh: row: 2 (over x), col: 16 (over z, y, core).
Axes of the slice: x: 2, y: 2, z: 4, core: 2. Of those that a mesh axis runs over, the one named last changes fastest.
Arguments:
- wave_field: float32 [64, 64, 16, 128], P(None, 'col', 'row'), may hold values from -6 to 6
- medium_term: float32 [64, 16, 128], P('col', 'row'), may hold values from 0.5 to 4
- node_flux: float32 [64, 16, 2, 384], P(None, 'col', 'row'), may hold values from -6 to 6
- node_cell: int32 [16, 2, 384], P('col', 'row'), may hold values from 0 to 4095
- block_target: int32 [16, 2, 16], P('col', 'row'), may hold values from 0 to 15, as said below
- boundary_matrix: bfloat16 [2, 1024, 12288], P(None, 'row', 'col'), may hold values from -0.078125 to 0.078125
Outputs:
- volume_image: float32 [64, 64, 16, 128], P(None, 'col', 'row')
- boundary_image: float32 [1024, 64], P(('row', 'col'))
The draws below stay inside these ranges and needn't reach their ends.
Inputs may be any that keep to these rules, and one draw needn't show every extreme that they name: For every brick (c, r), block_target[c, r, :] is a permutation of the 16 column blocks.
All inputs are finite; a program needn't handle non-finite values.
Results may differ from the reference program's by a relative error of at most 0.0029.
Values may be sent and summed in bfloat16 or wider, within the bound.
No kernel may reach another device: no remote copies, remote signals or barrier semaphores. Data moves between devices by JAX's collectives and lax.ppermute only.
A program may use at most 64 MiB of HBM per device.

```python
import math
import jax
import jax.numpy as jnp
from jax import lax

ANGLES = 32
COMP = 64
BRICK_X = 4
BRICK_Y = 8
BRICK_Z = 128
NODES_DEV = 384
SLAB_DEV = 512
COL_BLOCKS = 16
ROW_BLOCKS = 2
SLOT_NODES = 24
COL_NODES = 768
NODES = 12288
SLAB_ROWS = 1024
GRID_X = 64
GRID_Y = 16
GRID_Z = 128


def draw_block_target(key, part):
    key_list = jax.random.split(jax.random.fold_in(key, 11), COL_BLOCKS * ROW_BLOCKS)
    orders = jax.vmap(lambda single: jax.random.permutation(single, COL_BLOCKS))(key_list)
    return orders.reshape(COL_BLOCKS, ROW_BLOCKS, COL_BLOCKS).astype(jnp.int32)


def with_ends(array, own_key, smallest, high):
    longest = array.shape.index(max(array.shape))
    spots = []
    for shift in (0, 1):
        where = [jax.random.randint(jax.random.fold_in(own_key, axis), (), 0, length) for axis, length in enumerate(array.shape)]
        where[longest] = (where[longest] + shift) % array.shape[longest]
        spots.append(tuple(where))
    return array.at[spots[0]].set(smallest).at[spots[1]].set(high)


def strengthened(result, own_key, source, target, blocks, factor):
    owner, partner = [(jnp.arange(result.shape[axis_at]) // (result.shape[axis_at] // blocks)).reshape([-1 if axis == axis_at else 1 for axis in range(result.ndim)]) for axis_at in (source, target)]
    chosen = jax.random.permutation(own_key, blocks)[partner]
    strong = (owner == chosen) | (owner == (partner + blocks // 2) % blocks)
    return jnp.where(strong, factor * result, result)


def steps_of(rng, extent, cuts, low, largest):
    level, own = 1.0, jax.random.fold_in(rng, 6)
    for axis_at, blocks in cuts:
        steps = jnp.exp(jax.random.uniform(jax.random.fold_in(own, axis_at), (blocks,), jnp.float32, low / len(cuts), largest / len(cuts)))
        level = level * jnp.repeat(steps, extent[axis_at] // blocks).reshape([-1 if axis == axis_at else 1 for axis in range(len(extent))])
    return level


def centred(stream_key, dims, scale, reach, pieces=(), kind=jnp.bfloat16):
    drawn = jax.random.normal(stream_key, dims, jnp.float32) * scale
    if len(pieces) > 0:
        drawn = steps_of(stream_key, dims, pieces, -0.22, 0.18) * drawn
    return jnp.clip(drawn, min=-reach, max=reach).astype(kind)


def gaussian_with(stream_key, shape, deviation, limit, cuts, heavy, kind=jnp.bfloat16):
    drawn = deviation * jax.random.normal(stream_key, shape, jnp.float32)
    if cuts:
        drawn = drawn * steps_of(stream_key, shape, cuts, -0.22, 0.18)
    return jnp.clip(strengthened(drawn, jax.random.fold_in(stream_key, 3), *heavy), -limit, limit).astype(kind)


def setup_inputs(seed: int = 0) -> dict:
    streams_of = jax.random.split(jax.random.key(seed), 7)
    return {
        "wave_field": centred(streams_of[0], (COMP, GRID_X, GRID_Y, GRID_Z), 1.0, 6.0, ((1, 16), (2, 2)), jnp.float32),
        "medium_term": jnp.clip(jnp.exp(math.log(4.0) - 2.0794415 * jax.random.uniform(streams_of[1], (GRID_X, GRID_Y, GRID_Z), jnp.float32) ** steps_of(streams_of[1], (GRID_X, GRID_Y, GRID_Z), ((0, 16), (1, 2)), -0.2, 0.2)), 0.5, 4.0),
        "node_flux": centred(streams_of[2], (COMP, COL_BLOCKS, ROW_BLOCKS, NODES_DEV), 1.0, 6.0, ((1, 16), (2, 2)), jnp.float32),
        "node_cell": with_ends(jax.random.randint(streams_of[3], (COL_BLOCKS, ROW_BLOCKS, NODES_DEV), 0, BRICK_X * BRICK_Y * BRICK_Z), jax.random.fold_in(streams_of[3], 1), 0, (BRICK_X * BRICK_Y * BRICK_Z) - 1).astype(jnp.int32),
        "block_target": draw_block_target(jax.random.fold_in(streams_of[6], 71), 0),
        "boundary_matrix": gaussian_with(streams_of[5], (2, SLAB_ROWS, NODES), NODES ** -0.5, 0.078125, ((1, 2), (2, 16)), (2, 1, 16, 2.0)),
    }


stiff_weights = (8.0 / 3.0, 0.0, -1.0 / 6.0, -1.0 / 12.0)
mass_weights = (8.0 / 27.0, 4.0 / 27.0, 2.0 / 27.0, 1.0 / 27.0)


def apply_volume(values, medium_term):
    padded = jnp.pad(values, 1)
    width_x, width_y, depth_cells = values.shape
    stiffness = jnp.zeros_like(values)
    mass_sum = jnp.zeros_like(values)
    for offset_x in (-1, 0, 1):
        for offset_y in (-1, 0, 1):
            for offset_z in (-1, 0, 1):
                shifted = padded[1 + offset_x:1 + offset_x + width_x, 1 + offset_y:1 + offset_y + width_y, 1 + offset_z:1 + offset_z + depth_cells]
                distance = abs(offset_x) + abs(offset_y) + abs(offset_z)
                stiffness = stiffness + stiff_weights[distance] * shifted
                mass_sum = mass_sum + mass_weights[distance] * shifted
    return stiffness - medium_term * mass_sum


def reference(wave_field, medium_term, node_flux, node_cell, block_target, boundary_matrix):
    volume_image = lax.map(lambda single: apply_volume(single, medium_term), wave_field)
    brick_x = jnp.arange(COL_BLOCKS, dtype=jnp.int32)[:, None, None]
    brick_y = jnp.arange(ROW_BLOCKS, dtype=jnp.int32)[None, :, None]
    local_x = node_cell // (BRICK_Y * BRICK_Z)
    local_y = (node_cell // BRICK_Z) % BRICK_Y
    local_z = node_cell % BRICK_Z
    global_index = ((brick_x * BRICK_X + local_x) * GRID_Y + brick_y * BRICK_Y + local_y) * GRID_Z + local_z
    global_index = global_index.reshape(-1).astype(jnp.int32)
    flat_image = volume_image.reshape(COMP, -1)
    flat_image = flat_image.at[:, global_index].add(-node_flux.reshape(COMP, -1))
    volume_image = flat_image.reshape(COMP, GRID_X, GRID_Y, GRID_Z)
    flat_field = wave_field.reshape(COMP, -1)
    traces = flat_field[:, global_index].astype(jnp.bfloat16)
    node_index = jnp.arange(NODES_DEV, dtype=jnp.int32)
    slot_index = node_index // SLOT_NODES
    targets = block_target[:, :, slot_index]
    column = targets * COL_NODES + brick_y * NODES_DEV + brick_x * SLOT_NODES + (node_index % SLOT_NODES)[None, None, :]
    column = column.reshape(-1).astype(jnp.int32)
    trace_matrix = jnp.zeros((COMP, NODES), jnp.bfloat16).at[:, column].set(traces)
    trace_wide = trace_matrix.astype(jnp.float32)

    def block_rows(index):
        start = (index * SLAB_DEV).astype(jnp.int32)
        part_rows = lax.dynamic_slice_in_dim(boundary_matrix, start, SLAB_DEV, 1).astype(jnp.float32)
        products = jnp.dot(part_rows.reshape(2 * SLAB_DEV, NODES), trace_wide.T, preferred_element_type=jnp.float32)
        real_part = products[:SLAB_DEV]
        imag_part = products[SLAB_DEV:]
        return jnp.concatenate([real_part[:, :ANGLES] - imag_part[:, ANGLES:], imag_part[:, :ANGLES] + real_part[:, ANGLES:]], axis=1)

    blocks = lax.map(block_rows, jnp.arange(ROW_BLOCKS, dtype=jnp.int32))
    boundary_image = blocks.reshape(SLAB_ROWS, COMP)
    return volume_image, boundary_image
```

```python
import functools

import jax
import jax.numpy as jnp
from jax import lax
from jax.experimental import pallas as pl
from jax.experimental.pallas import tpu as pltpu
from jax.sharding import PartitionSpec as P

TILE_ROWS = 16
SMALL = 8 * 2**20


def vmem():
    return pl.BlockSpec(memory_space=pltpu.VMEM)


def one_hot_depth(cells, depth):
    lanes = jnp.bitwise_and(cells, depth - 1)
    at = lax.broadcasted_iota(jnp.int32, (depth, cells.shape[1]), 0)
    return jnp.where(at == lanes, 1.0, 0.0).astype(jnp.bfloat16)


def line_of(cells, depth):
    return jnp.right_shift(cells, depth.bit_length() - 1)


def trace_kernel(dims, target_ref, cell_ref, field_ref, tile_ref, *rest):
    comps, width_x, width_y, depth, rows, cols = dims
    face_refs, (lhs_ref,) = rest[:-1], rest[-1:]
    lines = width_x * width_y
    nodes = cell_ref.shape[1]
    slot_len = nodes // cols
    odd = lax.rem(lax.axis_index("row"), 2)
    for swap, face_ref in enumerate(face_refs):
        at_high = odd == swap
        layer = jnp.where(at_high, width_y - 1, 0)
        face_ref[...] = field_ref[pl.ds(layer, comps * width_x, stride=width_y), :]
    cells = cell_ref[...]
    hot = one_hot_depth(cells, depth)
    for line in range(lines):
        lhs_ref[pl.ds(line * comps, comps), :] = field_ref[
            pl.ds(line, comps, stride=lines), :
        ].astype(jnp.bfloat16)
    node_line = jnp.broadcast_to(line_of(cells, depth), (8, nodes))
    total = jnp.zeros((comps // 8, 8, nodes), jnp.float32)
    group = 4
    for first in range(0, lines, group):
        block = jnp.dot(
            lhs_ref[pl.ds(first * comps, group * comps), :], hot, preferred_element_type=jnp.float32
        ).reshape(group, comps // 8, 8, nodes)
        for line in range(group):
            total = jnp.where((node_line == first + line)[None], block[line], total)
    by_node = total.reshape(comps, nodes).T
    left_len = min(slot_len, TILE_ROWS)
    for slot in range(cols):
        piece = by_node[slot * slot_len : (slot + 1) * slot_len]
        left = piece[:left_len]
        right = piece[left_len:]
        if left_len < TILE_ROWS:
            left = jnp.concatenate(
                [left, jnp.zeros((TILE_ROWS - left_len, comps), jnp.float32)], axis=0
            )
        gap = TILE_ROWS - (slot_len - left_len)
        if slot_len == left_len:
            right = jnp.zeros((TILE_ROWS, comps), jnp.float32)
        elif gap:
            right = jnp.concatenate([right, jnp.zeros((gap, comps), jnp.float32)], axis=0)
        tile = jnp.concatenate([left, right], axis=1).astype(jnp.bfloat16)
        for row in range(rows):
            tile_ref[row * cols + target_ref[0, slot]] = tile


def face_kernel(dims, *refs):
    comps, width_x, width_y, depth, rows, cols = dims
    field_ref, row_refs, out_refs = refs[0], refs[1:-2], refs[-2:]
    odd = lax.rem(lax.axis_index("col"), 2)
    for swap, out_ref in enumerate(out_refs):
        layer = jnp.where(odd == swap, width_x - 1, 0)
        for comp in range(comps):
            start = pl.multiple_of(layer * width_y + comp * (width_x * width_y), width_y)
            out_ref[pl.ds(comp * width_y, width_y), :] = field_ref[pl.ds(start, width_y), :]
        for index, row_ref in enumerate(row_refs):
            out_ref[pl.ds(comps * width_y + index * comps, comps), :] = row_ref[
                pl.ds(layer, comps, stride=width_x), :
            ]


def unpack_tiles(tiles, slot_len, comps):
    left_len = min(slot_len, TILE_ROWS)
    parts = [tiles[:, :left_len, :comps]]
    if slot_len > left_len:
        parts.append(tiles[:, : slot_len - left_len, comps:])
    both = jnp.concatenate(parts, axis=1) if len(parts) > 1 else parts[0]
    return both.reshape(tiles.shape[0] * slot_len, comps)


def boundary_kernel(slot_len, own_rows, trace_ref, matrix_ref, out_ref):
    if len(trace_ref.shape) == 3:
        traces = unpack_tiles(
            trace_ref[...].astype(jnp.float32), slot_len, trace_ref.shape[2] // 2
        )
    else:
        traces = trace_ref[...].astype(jnp.float32)
    comps = traces.shape[1]
    angles = comps // 2
    turned = jnp.concatenate([-traces[:, angles:], traces[:, :angles]], axis=1)
    image = jnp.dot(
        matrix_ref[0], traces.astype(jnp.bfloat16), preferred_element_type=jnp.float32
    ) + jnp.dot(matrix_ref[1], turned.astype(jnp.bfloat16), preferred_element_type=jnp.float32)
    image = image.reshape(image.shape[0] // own_rows, own_rows, comps)
    half = own_rows // 2
    out_ref[...] = jnp.concatenate([image[:, :half], image[:, half:]], axis=2)


def sum_kernel(part_ref, out_ref):
    total = jnp.sum(part_ref[...], axis=0)
    half, lanes = total.shape
    out_ref[:half] = total[:, : lanes // 2]
    out_ref[half:] = total[:, lanes // 2 :]


def volume_kernel(dims, row_swaps, *refs):
    comps, width_x, width_y, depth, rows, cols = dims
    field_ref, medium_ref, flux_ref, cell_ref = refs[:4]
    row_refs = refs[4 : 4 + row_swaps]
    first_ref, second_ref = refs[4 + row_swaps : 6 + row_swaps]
    out_ref, lhs_ref, taken_ref = refs[6 + row_swaps :]
    lines = width_x * width_y
    nodes = cell_ref.shape[1]
    cells = cell_ref[...]
    hot = one_hot_depth(cells, depth)
    at_line = lax.broadcasted_iota(jnp.int32, (lines, nodes), 0)
    line_hot = jnp.where(at_line == line_of(cells, depth), 1.0, 0.0)

    for comp in range(comps):
        lhs_ref[pl.ds(comp * lines, lines), :] = (
            line_hot * jnp.broadcast_to(flux_ref[pl.ds(comp, 1), :], (lines, nodes))
        ).astype(jnp.bfloat16)
    chunk = 8 * lines

    def scatter(step, carry):
        here = pl.ds(pl.multiple_of(step * chunk, chunk), chunk)
        taken_ref[here, :] = lax.dot_general(
            lhs_ref[here, :], hot, (((1,), (1,)), ((), ())), preferred_element_type=jnp.float32
        )
        return carry

    lax.fori_loop(0, comps * lines // chunk, scatter, 0)

    row_odd = lax.rem(lax.axis_index("row"), 2) == 1
    col_odd = lax.rem(lax.axis_index("col"), 2) == 1
    shape = (width_y, depth)
    at_y = lax.broadcasted_iota(jnp.int32, shape, 0)
    at_z = lax.broadcasted_iota(jnp.int32, shape, 1)
    low_y, high_y = at_y == 0, at_y == width_y - 1
    low_z, high_z = at_z == 0, at_z == depth - 1
    weight = [1.0 / 12.0 + medium_ref[pl.ds(x * width_y, width_y), :] / 27.0 for x in range(width_x)]
    from_first = jnp.logical_or(
        jnp.logical_and(high_y, jnp.logical_not(row_odd)), jnp.logical_and(low_y, row_odd)
    )
    at_end = jnp.logical_or(low_y, high_y)

    def side_z(values):
        lower = jnp.where(low_z, 0.0, pltpu.roll(values, 1, 1))
        upper = jnp.where(high_z, 0.0, pltpu.roll(values, depth - 1, 1))
        return lower + upper

    def side_y(values, ends):
        lower = jnp.where(low_y, ends, pltpu.roll(values, 1, 0))
        upper = jnp.where(high_y, ends, pltpu.roll(values, width_y - 1, 0))
        return lower + upper

    def wide(ref, index):
        return jnp.broadcast_to(ref[pl.ds(index, 1), :], shape)

    def ends_of(first, second):
        if second is None:
            return jnp.where(from_first, first, 0.0)
        return jnp.where(from_first, first, second)

    def component(comp, carry):
        base = comp * lines
        planes = [
            field_ref[pl.ds(pl.multiple_of(base + x * width_y, width_y), width_y), :]
            for x in range(width_x)
        ]
        face = pl.ds(pl.multiple_of(comp * width_y, width_y), width_y)
        first, second = first_ref[face, :], second_ref[face, :]
        planes = (
            [jnp.where(col_odd, first, second)] + planes + [jnp.where(col_odd, second, first)]
        )
        ends = []
        tail = comps * width_y
        for index in range(row_swaps):
            inner = [wide(row_refs[index], comp * width_x + x) for x in range(width_x)]
            corner_first = wide(first_ref, tail + index * comps + comp)
            corner_second = wide(second_ref, tail + index * comps + comp)
            ends.append(
                [jnp.where(col_odd, corner_first, corner_second)]
                + inner
                + [jnp.where(col_odd, corner_second, corner_first)]
            )
        ends = [
            ends_of(ends[0][x], ends[1][x] if row_swaps > 1 else None) for x in range(width_x + 2)
        ]
        for x in range(width_x):
            centre = planes[x + 1]
            sides = planes[x] + planes[x + 2]
            over_x = 2.0 * centre + sides
            ends_x = 2.0 * ends[x + 1] + (ends[x] + ends[x + 2])
            over_xy = 2.0 * over_x + side_y(over_x, ends_x)
            over_xyz = 2.0 * over_xy + side_z(over_xy)
            near = sides + side_y(centre, ends[x + 1]) + side_z(centre)
            here = pl.ds(pl.multiple_of(base + x * width_y, width_y), width_y)
            out_ref[here, :] = (
                (10.0 / 3.0) * centre
                + (1.0 / 3.0) * near
                - weight[x] * over_xyz
                - taken_ref[here, :]
            )
        return carry

    lax.fori_loop(0, comps, component, 0, unroll=4)


def swap_pairs(count, swap):
    pairs = []
    for low in range(swap, count - 1, 2):
        pairs += [(low, low + 1), (low + 1, low)]
    return pairs


def on_device(wave_field, medium_term, node_flux, node_cell, block_target, boundary_matrix):
    comps, width_x, width_y, depth = wave_field.shape
    rows, cols = lax.axis_size("row"), lax.axis_size("col")
    dims = (comps, width_x, width_y, depth, rows, cols)
    lines = width_x * width_y
    nodes = node_cell.shape[-1]
    slot_len = nodes // cols
    row_swaps = 1 if rows == 2 else 2
    slab_rows, span = boundary_matrix.shape[1:]
    own_rows = slab_rows // cols
    f32, bf16 = jnp.float32, jnp.bfloat16
    params = pltpu.CompilerParams(vmem_limit_bytes=SMALL)

    field = wave_field.reshape(comps * lines, depth)
    cells = node_cell.reshape(1, nodes)
    targets = block_target.reshape(1, cols)
    flux = node_flux.reshape(comps, nodes)
    medium = medium_term.reshape(lines, depth)

    tiles, *faces = pl.pallas_call(
        functools.partial(trace_kernel, dims),
        out_shape=[jax.ShapeDtypeStruct((rows * cols, TILE_ROWS, 2 * comps), bf16)]
        + [jax.ShapeDtypeStruct((comps * width_x, depth), f32)] * row_swaps,
        in_specs=[pl.BlockSpec(memory_space=pltpu.SMEM), vmem(), vmem()],
        out_specs=[vmem()] * (1 + row_swaps),
        scratch_shapes=[pltpu.VMEM((comps * lines, depth), bf16)],
        compiler_params=params,
        name="traces",
    )(targets, cells, field)

    row_sides = [
        lax.ppermute(face, "row", swap_pairs(rows, swap)) for swap, face in enumerate(faces)
    ]
    received = lax.all_to_all(tiles, ("row", "col"), 0, 0, tiled=True)

    col_faces = pl.pallas_call(
        functools.partial(face_kernel, dims),
        out_shape=[jax.ShapeDtypeStruct((comps * (width_y + row_swaps), depth), f32)] * 2,
        in_specs=[vmem()] * (1 + row_swaps),
        out_specs=[vmem()] * 2,
        compiler_params=params,
        name="faces",
    )(field, *row_sides)
    col_sides = [
        lax.ppermute(face, "col", swap_pairs(cols, swap)) for swap, face in enumerate(col_faces)
    ]

    if slot_len % 8:
        received = unpack_tiles(received, slot_len, comps)
    shares = pl.pallas_call(
        functools.partial(boundary_kernel, slot_len, own_rows),
        out_shape=jax.ShapeDtypeStruct((cols, own_rows // 2, 2 * comps), f32),
        in_specs=[vmem()] * 2,
        out_specs=vmem(),
        compiler_params=pltpu.CompilerParams(vmem_limit_bytes=2 * SMALL),
        name="boundary",
    )(received, boundary_matrix)
    shares = lax.all_to_all(shares, "col", 0, 0, tiled=True)

    volume = pl.pallas_call(
        functools.partial(volume_kernel, dims, row_swaps),
        out_shape=jax.ShapeDtypeStruct((comps * lines, depth), f32),
        in_specs=[vmem()] * (6 + row_swaps),
        out_specs=vmem(),
        scratch_shapes=[
            pltpu.VMEM((comps * lines, nodes), bf16),
            pltpu.VMEM((comps * lines, depth), f32),
        ],
        compiler_params=params,
        name="volume",
    )(field, medium, flux, cells, *row_sides, *col_sides)

    boundary_image = pl.pallas_call(
        sum_kernel,
        out_shape=jax.ShapeDtypeStruct((own_rows, comps), f32),
        in_specs=[vmem()],
        out_specs=vmem(),
        compiler_params=params,
        name="sum",
    )(shares)
    return (volume.reshape(comps, width_x, width_y, depth), boundary_image)


def solution(mesh):
    in_specs = (
        P(None, "col", "row", None),
        P("col", "row", None),
        P(None, "col", "row", None),
        P("col", "row", None),
        P("col", "row", None),
        P(None, "row", "col"),
    )
    out_specs = (P(None, "col", "row", None), P(("row", "col"), None))
    return jax.shard_map(
        on_device, mesh=mesh, in_specs=in_specs, out_specs=out_specs, check_vma=False
    )
```

```python
import functools

import jax
import jax.numpy as jnp
from jax import lax
from jax.experimental import pallas as pl
from jax.experimental.pallas import tpu as pltpu
from jax.sharding import PartitionSpec as P

TILE_ROWS = 16
SMALL = 8 * 2**20
WHOLE = 64560 * 2**10


def vmem():
    return pl.BlockSpec(memory_space=pltpu.VMEM)


def hbm():
    return pl.BlockSpec(memory_space=pltpu.HBM)


def one_hot_depth(cells, depth):
    lanes = jnp.bitwise_and(cells, depth - 1)
    at = lax.broadcasted_iota(jnp.int32, (depth, cells.shape[1]), 0)
    return jnp.where(at == lanes, 1.0, 0.0).astype(jnp.bfloat16)


def line_of(cells, depth):
    return jnp.right_shift(cells, depth.bit_length() - 1)


def trace_kernel(dims, row_swaps, target_hbm, cell_hbm, field_hbm, tile_ref, *rest):
    comps, width_x, width_y, depth, rows, cols = dims
    row_faces, col_faces = rest[:row_swaps], rest[row_swaps : row_swaps + 2]
    target_ref, cell_ref, field_ref, lhs_ref, arrived, left_sem = rest[row_swaps + 2 :]
    lines = width_x * width_y
    nodes = cell_ref.shape[1]
    slot_len = nodes // cols
    copies = [
        pltpu.make_async_copy(source, target, arrived.at[index])
        for index, (source, target) in enumerate(
            [(cell_hbm, cell_ref), (field_hbm, field_ref), (target_hbm, target_ref)]
        )
    ]
    for copy in copies:
        copy.start()
    copies[0].wait()
    cells = cell_ref[...]
    hot = one_hot_depth(cells, depth)
    node_line = jnp.broadcast_to(line_of(cells, depth), (8, nodes))
    copies[1].wait()
    col_odd = lax.rem(lax.axis_index("col"), 2)
    sent = []
    for swap, face_ref in enumerate(col_faces):
        layer = jnp.where(col_odd == swap, width_x - 1, 0)
        start = pl.multiple_of(layer * width_y, width_y)
        sent.append(
            pltpu.make_async_copy(
                field_ref.at[:, pl.ds(start, width_y), :], face_ref, left_sem.at[swap]
            )
        )
        sent[-1].start()
    flat = field_ref.reshape(comps * lines, depth)
    for line in range(lines):
        lhs_ref[pl.ds(line * comps, comps), :] = flat[
            pl.ds(line, comps, stride=lines), :
        ].astype(jnp.bfloat16)
    total = jnp.zeros((comps // 8, 8, nodes), jnp.float32)
    group = 4
    for first in range(0, lines, group):
        block = jnp.dot(
            lhs_ref[pl.ds(first * comps, group * comps), :], hot, preferred_element_type=jnp.float32
        ).reshape(group, comps // 8, 8, nodes)
        for line in range(group):
            total = jnp.where((node_line == first + line)[None], block[line], total)
    by_node = total.reshape(comps, nodes).T
    copies[2].wait()
    left_len = min(slot_len, TILE_ROWS)
    for slot in range(cols):
        piece = by_node[slot * slot_len : (slot + 1) * slot_len]
        left = piece[:left_len]
        right = piece[left_len:]
        if left_len < TILE_ROWS:
            left = jnp.concatenate(
                [left, jnp.zeros((TILE_ROWS - left_len, comps), jnp.float32)], axis=0
            )
        gap = TILE_ROWS - (slot_len - left_len)
        if slot_len == left_len:
            right = jnp.zeros((TILE_ROWS, comps), jnp.float32)
        elif gap:
            right = jnp.concatenate([right, jnp.zeros((gap, comps), jnp.float32)], axis=0)
        tile = jnp.concatenate([left, right], axis=1).astype(jnp.bfloat16)
        for row in range(rows):
            tile_ref[row * cols + target_ref[0, slot]] = tile
    row_odd = lax.rem(lax.axis_index("row"), 2)
    for swap, face_ref in enumerate(row_faces):
        layer = jnp.where(row_odd == swap, width_y - 1, 0)
        face_ref[...] = flat[pl.ds(layer, comps * width_x, stride=width_y), :]
    for copy in sent:
        copy.wait()


def corner_kernel(dims, row_swaps, *refs):
    comps, width_x = dims[:2]
    odd = lax.rem(lax.axis_index("col"), 2)
    for swap, out_ref in enumerate(refs[row_swaps:]):
        layer = jnp.where(odd == swap, width_x - 1, 0)
        for index, row_ref in enumerate(refs[:row_swaps]):
            out_ref[pl.ds(index * comps, comps), :] = row_ref[
                pl.ds(layer, comps, stride=width_x), :
            ]


def unpack_tiles(tiles, slot_len, comps):
    left_len = min(slot_len, TILE_ROWS)
    parts = [tiles[:, :left_len, :comps]]
    if slot_len > left_len:
        parts.append(tiles[:, : slot_len - left_len, comps:])
    both = jnp.concatenate(parts, axis=1) if len(parts) > 1 else parts[0]
    return both.reshape(tiles.shape[0] * slot_len, comps)


def boundary_kernel(slot_len, own_rows, trace_ref, real_ref, imag_ref, corner_ref, out_ref):
    if len(trace_ref.shape) == 3:
        traces = unpack_tiles(
            trace_ref[...].astype(jnp.float32), slot_len, trace_ref.shape[2] // 2
        )
    else:
        traces = trace_ref[...].astype(jnp.float32)
    comps = traces.shape[1]
    angles = comps // 2
    turned = jnp.concatenate([-traces[:, angles:], traces[:, :angles]], axis=1)
    image = jnp.dot(
        real_ref[...], traces.astype(jnp.bfloat16), preferred_element_type=jnp.float32
    ) + jnp.dot(imag_ref[...], turned.astype(jnp.bfloat16), preferred_element_type=jnp.float32)
    image = image.reshape(image.shape[0] // own_rows, own_rows, comps)
    half = own_rows // 2
    out_ref[...] = jnp.concatenate([image[:, :half], image[:, half:]], axis=2)


def shifted_z(values, step):
    rows, depth = values.shape
    at_z = lax.broadcasted_iota(jnp.int32, (rows, depth), 1)
    outside = at_z == (0 if step == 1 else depth - 1)
    return jnp.where(outside, 0.0, pltpu.roll(values, step % depth, 1))


def side_z(values):
    return shifted_z(values, 1) + shifted_z(values, -1)


def volume_kernel(dims, row_swaps, *refs):
    comps, width_x, width_y, depth, rows, cols = dims
    field_ref, medium_ref, flux_ref, cell_ref = refs[:4]
    row_refs = refs[4 : 4 + row_swaps]
    first_ref, second_ref = refs[4 + row_swaps : 6 + row_swaps]
    out_ref, edge_ref, lhs_ref, taken_ref = refs[6 + row_swaps :]
    lines = width_x * width_y
    nodes = cell_ref.shape[1]
    cells = cell_ref[...]
    hot = one_hot_depth(cells, depth)
    at_line = lax.broadcasted_iota(jnp.int32, (lines, nodes), 0)
    line_hot = jnp.where(at_line == line_of(cells, depth), 1.0, 0.0)

    for comp in range(comps):
        lhs_ref[pl.ds(comp * lines, lines), :] = (
            line_hot * jnp.broadcast_to(flux_ref[pl.ds(comp, 1), :], (lines, nodes))
        ).astype(jnp.bfloat16)
    taken_ref[...] = lax.dot_general(
        lhs_ref[...], hot, (((1,), (1,)), ((), ())), preferred_element_type=jnp.float32
    )

    row_odd = lax.rem(lax.axis_index("row"), 2) == 1
    col_odd = lax.rem(lax.axis_index("col"), 2) == 1
    shape = (width_y, depth)
    at_y = lax.broadcasted_iota(jnp.int32, shape, 0)
    low_y, high_y = at_y == 0, at_y == width_y - 1
    weight = [1.0 / 12.0 + medium_ref[pl.ds(x * width_y, width_y), :] / 27.0 for x in range(width_x)]
    from_first = jnp.logical_or(
        jnp.logical_and(high_y, jnp.logical_not(row_odd)), jnp.logical_and(low_y, row_odd)
    )

    def side_y(values, ends):
        lower = jnp.where(low_y, ends, pltpu.roll(values, 1, 0))
        upper = jnp.where(high_y, ends, pltpu.roll(values, width_y - 1, 0))
        return lower + upper

    def wide(ref, index):
        return jnp.broadcast_to(ref[pl.ds(index, 1), :], shape)

    def component(comp):
        base = comp * lines
        planes = [
            field_ref[pl.ds(pl.multiple_of(base + x * width_y, width_y), width_y), :]
            for x in range(width_x)
        ]
        face = pl.ds(pl.multiple_of(comp * width_y, width_y), width_y)
        first, second = first_ref[face, :], second_ref[face, :]
        planes = (
            [jnp.where(col_odd, first, second)] + planes + [jnp.where(col_odd, second, first)]
        )
        ends = []
        for x in range(width_x):
            line = [wide(row_ref, comp * width_x + x) for row_ref in row_refs]
            ends.append(jnp.where(from_first, line[0], line[1] if row_swaps > 1 else 0.0))
        none = jnp.zeros(shape, jnp.float32)
        ends = [none] + ends + [none]
        for x in range(width_x):
            centre = planes[x + 1]
            sides = planes[x] + planes[x + 2]
            over_x = 2.0 * centre + sides
            ends_x = 2.0 * ends[x + 1] + (ends[x] + ends[x + 2])
            over_xy = 2.0 * over_x + side_y(over_x, ends_x)
            over_xyz = 2.0 * over_xy + side_z(over_xy)
            near = sides + side_y(centre, ends[x + 1]) + side_z(centre)
            here = pl.ds(pl.multiple_of(base + x * width_y, width_y), width_y)
            image = (
                (10.0 / 3.0) * centre
                + (1.0 / 3.0) * near
                - weight[x] * over_xyz
                - taken_ref[here, :]
            )
            out_ref[here, :] = image
            for side in range(2):
                if x == side * (width_x - 1):
                    edge_ref[side, face, :] = image

    together = 16

    def components(step, carry):
        for index in range(together):
            component(step * together + index)
        return carry

    lax.fori_loop(0, comps // together, components, 0)


def last_kernel(
    dims, row_swaps, part_ref, medium_ref, edge_ref, first_ref, second_ref, *refs
):
    comps, width_x, width_y, depth, rows, cols = dims
    image_ref, volume_ref, plane_ref, total_ref, sent = refs[1:]
    row_odd = lax.rem(lax.axis_index("row"), 2)
    col_odd = lax.rem(lax.axis_index("col"), 2) == 1
    copies = []
    for side in range(2):
        at_x = side * (width_x - 1)
        plane_ref[side] = edge_ref[side]
        for index in range(row_swaps):
            lines = pl.ds(index * comps, comps)
            first, second = first_ref[lines, :], second_ref[lines, :]
            if side:
                line = jnp.where(col_odd, second, first)
            else:
                line = jnp.where(col_odd, first, second)
            at_y = jnp.where(row_odd == index, width_y - 1, 0)
            weight = 1.0 / 12.0 + medium_ref[pl.ds(at_x * width_y + at_y, 1), :] / 27.0
            here = pl.ds(at_y, comps, stride=width_y)
            plane_ref[side, here, :] = plane_ref[side, here, :] - weight * (
                2.0 * line + side_z(line)
            )
        copies.append(
            pltpu.make_async_copy(
                plane_ref.at[side].reshape(comps, width_y, depth),
                volume_ref.at[:, pl.ds(at_x * width_y, width_y), :],
                sent.at[side],
            )
        )
        copies[-1].start()
    total = jnp.sum(part_ref[...], axis=0)
    half, lanes = total.shape
    total_ref[:half] = total[:, : lanes // 2]
    total_ref[half:] = total[:, lanes // 2 :]
    copies.append(pltpu.make_async_copy(total_ref, image_ref, sent.at[2]))
    copies[-1].start()
    for copy in copies:
        copy.wait()


def swap_pairs(count, swap):
    pairs = []
    for low in range(swap, count - 1, 2):
        pairs += [(low, low + 1), (low + 1, low)]
    return pairs


def on_device(wave_field, medium_term, node_flux, node_cell, block_target, boundary_matrix):
    comps, width_x, width_y, depth = wave_field.shape
    rows, cols = lax.axis_size("row"), lax.axis_size("col")
    dims = (comps, width_x, width_y, depth, rows, cols)
    lines = width_x * width_y
    nodes = node_cell.shape[-1]
    slot_len = nodes // cols
    row_swaps = 1 if rows == 2 else 2
    slab_rows, span = boundary_matrix.shape[1:]
    own_rows = slab_rows // cols
    f32, bf16 = jnp.float32, jnp.bfloat16
    params = pltpu.CompilerParams(vmem_limit_bytes=SMALL)
    whole_params = pltpu.CompilerParams(vmem_limit_bytes=WHOLE)

    field = wave_field.reshape(comps * lines, depth)
    cells = node_cell.reshape(1, nodes)
    targets = block_target.reshape(1, cols)
    flux = node_flux.reshape(comps, nodes)
    medium = medium_term.reshape(lines, depth)

    tiles, *faces = pl.pallas_call(
        functools.partial(trace_kernel, dims, row_swaps),
        out_shape=[jax.ShapeDtypeStruct((rows * cols, TILE_ROWS, 2 * comps), bf16)]
        + [jax.ShapeDtypeStruct((comps * width_x, depth), f32)] * row_swaps
        + [jax.ShapeDtypeStruct((comps, width_y, depth), f32)] * 2,
        in_specs=[hbm()] * 3,
        out_specs=[vmem()] * (1 + row_swaps) + [hbm()] * 2,
        scratch_shapes=[
            pltpu.SMEM((1, cols), jnp.int32),
            pltpu.VMEM((1, nodes), jnp.int32),
            pltpu.VMEM((comps, lines, depth), f32),
            pltpu.VMEM((comps * lines, depth), bf16),
            pltpu.SemaphoreType.DMA((3,)),
            pltpu.SemaphoreType.DMA((2,)),
        ],
        compiler_params=whole_params,
        name="traces",
    )(targets, cells, field.reshape(comps, lines, depth))
    col_sides = [
        lax.ppermute(face, "col", swap_pairs(cols, swap)).reshape(comps * width_y, depth)
        for swap, face in enumerate(faces[row_swaps:])
    ]
    row_sides = [
        lax.ppermute(face, "row", swap_pairs(rows, swap))
        for swap, face in enumerate(faces[:row_swaps])
    ]
    received = lax.all_to_all(tiles, ("row", "col"), 0, 0, tiled=True)

    if slot_len % 8:
        received = unpack_tiles(received, slot_len, comps)
    corners = pl.pallas_call(
        functools.partial(corner_kernel, dims, row_swaps),
        out_shape=[jax.ShapeDtypeStruct((row_swaps * comps, depth), f32)] * 2,
        in_specs=[vmem()] * row_swaps,
        out_specs=[vmem()] * 2,
        compiler_params=params,
        name="corners",
    )(*row_sides)
    shares = pl.pallas_call(
        functools.partial(boundary_kernel, slot_len, own_rows),
        out_shape=jax.ShapeDtypeStruct((cols, own_rows // 2, 2 * comps), f32),
        in_specs=[vmem()] * 4,
        out_specs=vmem(),
        compiler_params=params,
        name="boundary",
    )(received, boundary_matrix[0], boundary_matrix[1], corners[0])
    corner_sides = [
        lax.ppermute(lines_of, "col", swap_pairs(cols, swap))
        for swap, lines_of in enumerate(corners)
    ]
    shares = lax.all_to_all(shares, "col", 0, 0, tiled=True)

    volume, edges = pl.pallas_call(
        functools.partial(volume_kernel, dims, row_swaps),
        out_shape=[
            jax.ShapeDtypeStruct((comps * lines, depth), f32),
            jax.ShapeDtypeStruct((2, comps * width_y, depth), f32),
        ],
        in_specs=[vmem()] * (6 + row_swaps),
        out_specs=[vmem()] * 2,
        scratch_shapes=[
            pltpu.VMEM((comps * lines, nodes), bf16),
            pltpu.VMEM((comps * lines, depth), f32),
        ],
        compiler_params=params,
        name="volume",
    )(field, medium, flux, cells, *row_sides, *col_sides)

    boundary_image, volume = pl.pallas_call(
        functools.partial(last_kernel, dims, row_swaps),
        out_shape=[
            jax.ShapeDtypeStruct((own_rows, comps), f32),
            jax.ShapeDtypeStruct((comps, lines, depth), f32),
        ],
        in_specs=[vmem()] * 5 + [hbm()],
        out_specs=[hbm(), hbm()],
        scratch_shapes=[
            pltpu.VMEM((2, comps * width_y, depth), f32),
            pltpu.VMEM((own_rows, comps), f32),
            pltpu.SemaphoreType.DMA((3,)),
        ],
        input_output_aliases={5: 1},
        compiler_params=params,
        name="last",
    )(shares, medium, edges, *corner_sides, volume.reshape(comps, lines, depth))
    return (volume.reshape(comps, width_x, width_y, depth), boundary_image)


def solution(mesh):
    in_specs = (
        P(None, "col", "row", None),
        P("col", "row", None),
        P(None, "col", "row", None),
        P("col", "row", None),
        P("col", "row", None),
        P(None, "row", "col"),
    )
    out_specs = (P(None, "col", "row", None), P(("row", "col"), None))
    return jax.shard_map(
        on_device, mesh=mesh, in_specs=in_specs, out_specs=out_specs, check_vma=False
    )
```

```python
import functools

import jax
import jax.numpy as jnp
from jax import lax
from jax.experimental import pallas as pl
from jax.experimental.pallas import tpu as pltpu
from jax.sharding import PartitionSpec as P

TILE_ROWS = 16
SMALL = 8 * 2**20
WHOLE = 64560 * 2**10


def vmem():
    return pl.BlockSpec(memory_space=pltpu.VMEM)


def hbm():
    return pl.BlockSpec(memory_space=pltpu.HBM)


def folded_hot(cells, depth, lines, fold):
    few = lines // fold
    line = jnp.right_shift(cells, depth.bit_length() - 1)
    own = jnp.bitwise_and(line, few - 1)
    key = jnp.right_shift(line, few.bit_length() - 1) * depth + jnp.bitwise_and(cells, depth - 1)
    at = lax.broadcasted_iota(jnp.int32, (fold * depth, cells.shape[1]), 0)
    return jnp.where(at == key, 1.0, 0.0).astype(jnp.bfloat16), own


def root_first(count):
    root = count * 11 // 16
    return [root] + [index for index in range(count) if index != root]


def trace_kernel(dims, row_swaps, target_hbm, cell_hbm, field_hbm, tile_hbm, *rest):
    comps, width_x, width_y, depth, rows, cols = dims
    row_faces, col_faces = rest[:row_swaps], rest[row_swaps : row_swaps + 2]
    target_ref, cell_ref, field_ref, lhs_ref, tile_ref, side_ref, arrived, left_sem = rest[
        row_swaps + 2 :
    ]
    lines = width_x * width_y
    nodes = cell_ref.shape[1]
    slot_len = nodes // cols
    chunks, few = lhs_ref.shape[:2]
    fold = lines // few
    span = comps // chunks
    copies = [pltpu.make_async_copy(cell_hbm, cell_ref, arrived.at[chunks])]
    for chunk in range(chunks):
        part = pl.ds(chunk * span, span)
        copies.append(
            pltpu.make_async_copy(field_hbm.at[part], field_ref.at[part], arrived.at[chunk])
        )
    copies.append(pltpu.make_async_copy(target_hbm, target_ref, arrived.at[chunks + 1]))
    for copy in copies:
        copy.start()
    sent = []
    copies[0].wait()
    hot, own = folded_hot(cell_ref[...], depth, lines, fold)
    own = jnp.broadcast_to(own, (8, nodes))
    flat = field_ref.reshape(comps * lines, depth)
    found = []
    for chunk in range(chunks):
        copies[1 + chunk].wait()
        for line in range(lines):
            lhs_ref[chunk, line % few, :, pl.ds(line // few * depth, depth)] = flat[
                pl.ds(chunk * span * lines + line, span, stride=lines), :
            ].astype(jnp.bfloat16)
        total = jnp.zeros((span // 8, 8, nodes), jnp.float32)
        group = min(4, few)
        for first in range(0, few, group):
            block = jnp.dot(
                lhs_ref[chunk, first : first + group].reshape(group * span, fold * depth),
                hot,
                preferred_element_type=jnp.float32,
            ).reshape(group, span // 8, 8, nodes)
            for line in range(group):
                total = jnp.where((own == first + line)[None], block[line], total)
        found.append(total.reshape(span, nodes))
    col_odd = lax.rem(lax.axis_index("col"), 2)
    for swap, face_ref in enumerate(col_faces):
        layer = jnp.where(col_odd == swap, width_x - 1, 0)
        start = pl.multiple_of(layer * width_y, width_y)
        sent.append(
            pltpu.make_async_copy(
                field_ref.at[:, pl.ds(start, width_y), :], face_ref, left_sem.at[swap]
            )
        )
        sent[-1].start()
    row_odd = lax.rem(lax.axis_index("row"), 2)
    for swap, face_ref in enumerate(row_faces):
        layer = jnp.where(row_odd == swap, width_y - 1, 0)
        side_ref[swap] = flat[pl.ds(layer, comps * width_x, stride=width_y), :]
        sent.append(pltpu.make_async_copy(side_ref.at[swap], face_ref, left_sem.at[2 + swap]))
        sent[-1].start()
    by_node = jnp.concatenate(found, axis=0).T
    copies[-1].wait()
    left_len = min(slot_len, TILE_ROWS)
    for slot in range(cols):
        piece = by_node[slot * slot_len : (slot + 1) * slot_len]
        left = piece[:left_len]
        right = piece[left_len:]
        if left_len < TILE_ROWS:
            left = jnp.concatenate(
                [left, jnp.zeros((TILE_ROWS - left_len, comps), jnp.float32)], axis=0
            )
        gap = TILE_ROWS - (slot_len - left_len)
        if slot_len == left_len:
            right = jnp.zeros((TILE_ROWS, comps), jnp.float32)
        elif gap:
            right = jnp.concatenate([right, jnp.zeros((gap, comps), jnp.float32)], axis=0)
        tile = jnp.concatenate([left, right], axis=1).astype(jnp.bfloat16)
        for row in range(rows):
            tile_ref[row * cols + target_ref[0, slot]] = tile
    sent.append(pltpu.make_async_copy(tile_ref, tile_hbm, left_sem.at[2 + row_swaps]))
    sent[-1].start()
    for copy in sent:
        copy.wait()


def corner_kernel(dims, first_ref, second_ref, *out_refs):
    comps, width_x, width_y = dims[:3]
    odd = lax.rem(lax.axis_index("row"), 2)
    for swap, out_ref in enumerate(out_refs):
        layer = jnp.where(odd == swap, width_y - 1, 0)
        for index, ref in enumerate((first_ref, second_ref)):
            out_ref[pl.ds(index * comps, comps), :] = ref[pl.ds(layer, comps, stride=width_y), :]


def unpack_tiles(tiles, slot_len, comps):
    left_len = min(slot_len, TILE_ROWS)
    parts = [tiles[:, :left_len, :comps]]
    if slot_len > left_len:
        parts.append(tiles[:, : slot_len - left_len, comps:])
    both = jnp.concatenate(parts, axis=1) if len(parts) > 1 else parts[0]
    return both.reshape(tiles.shape[0] * slot_len, comps)


def boundary_kernel(slot_len, own_rows, trace_ref, real_ref, imag_ref, row_ref, out_ref):
    if len(trace_ref.shape) == 3:
        traces = unpack_tiles(
            trace_ref[...].astype(jnp.float32), slot_len, trace_ref.shape[2] // 2
        )
    else:
        traces = trace_ref[...].astype(jnp.float32)
    comps = traces.shape[1]
    angles = comps // 2
    turned = jnp.concatenate([-traces[:, angles:], traces[:, :angles]], axis=1)
    image = jnp.dot(
        real_ref[...], traces.astype(jnp.bfloat16), preferred_element_type=jnp.float32
    ) + jnp.dot(imag_ref[...], turned.astype(jnp.bfloat16), preferred_element_type=jnp.float32)
    image = image.reshape(image.shape[0] // own_rows, own_rows, comps)
    half = own_rows // 2
    packed = jnp.concatenate([image[:, :half], image[:, half:]], axis=2)
    for place, col in enumerate(root_first(packed.shape[0])):
        out_ref[place] = packed[col]


def shifted_z(values, step):
    rows, depth = values.shape
    at_z = lax.broadcasted_iota(jnp.int32, (rows, depth), 1)
    outside = at_z == (0 if step == 1 else depth - 1)
    return jnp.where(outside, 0.0, pltpu.roll(values, step % depth, 1))


def side_z(values):
    return shifted_z(values, 1) + shifted_z(values, -1)


def volume_kernel(dims, row_swaps, *refs):
    comps, width_x, width_y, depth, rows, cols = dims
    field_ref, medium_ref, flux_ref, cell_ref = refs[:4]
    row_refs = refs[4 : 4 + row_swaps]
    first_ref, second_ref = refs[4 + row_swaps : 6 + row_swaps]
    out_ref, edge_ref, lhs_ref, taken_ref = refs[6 + row_swaps :]
    lines = width_x * width_y
    nodes = cell_ref.shape[1]
    fold = 2
    few = lines // fold
    hot, own = folded_hot(cell_ref[...], depth, lines, fold)
    at_line = lax.broadcasted_iota(jnp.int32, (few, nodes), 0)
    line_hot = jnp.where(at_line == own, 1.0, 0.0)
    for comp in range(comps):
        lhs_ref[pl.ds(comp * few, few), :] = (
            line_hot * jnp.broadcast_to(flux_ref[comp], (few, nodes))
        ).astype(jnp.bfloat16)
    taken_ref[...] = lax.dot_general(
        lhs_ref[...], hot, (((1,), (1,)), ((), ())), preferred_element_type=jnp.float32
    )

    row_odd = lax.rem(lax.axis_index("row"), 2) == 1
    col_odd = lax.rem(lax.axis_index("col"), 2) == 1
    shape = (width_y, depth)
    at_y = lax.broadcasted_iota(jnp.int32, shape, 0)
    low_y, high_y = at_y == 0, at_y == width_y - 1
    weight = [1.0 / 12.0 + medium_ref[pl.ds(x * width_y, width_y), :] / 27.0 for x in range(width_x)]
    from_first = jnp.logical_or(
        jnp.logical_and(high_y, jnp.logical_not(row_odd)), jnp.logical_and(low_y, row_odd)
    )

    def side_y(values, ends):
        lower = jnp.where(low_y, ends, pltpu.roll(values, 1, 0))
        upper = jnp.where(high_y, ends, pltpu.roll(values, width_y - 1, 0))
        return lower + upper

    def wide(ref, index):
        return jnp.broadcast_to(ref[pl.ds(index, 1), :], shape)

    def component(comp):
        base = comp * lines
        planes = [
            field_ref[pl.ds(pl.multiple_of(base + x * width_y, width_y), width_y), :]
            for x in range(width_x)
        ]
        face = pl.ds(pl.multiple_of(comp * width_y, width_y), width_y)
        first, second = first_ref[face, :], second_ref[face, :]
        planes = (
            [jnp.where(col_odd, first, second)] + planes + [jnp.where(col_odd, second, first)]
        )
        ends = []
        for x in range(width_x):
            line = [wide(row_ref, comp * width_x + x) for row_ref in row_refs]
            ends.append(jnp.where(from_first, line[0], line[1] if row_swaps > 1 else 0.0))
        none = jnp.zeros(shape, jnp.float32)
        ends = [none] + ends + [none]
        for x in range(width_x):
            centre = planes[x + 1]
            sides = planes[x] + planes[x + 2]
            over_x = 2.0 * centre + sides
            ends_x = 2.0 * ends[x + 1] + (ends[x] + ends[x + 2])
            over_xy = 2.0 * over_x + side_y(over_x, ends_x)
            over_xyz = 2.0 * over_xy + side_z(over_xy)
            near = sides + side_y(centre, ends[x + 1]) + side_z(centre)
            here = pl.ds(pl.multiple_of(base + x * width_y, width_y), width_y)
            image = (
                (10.0 / 3.0) * centre
                + (1.0 / 3.0) * near
                - weight[x] * over_xyz
                - taken_ref[
                    pl.ds(
                        pl.multiple_of(comp * few + x * width_y % few, width_y), width_y
                    ),
                    pl.ds(x * width_y // few * depth, depth),
                ]
            )
            out_ref[here, :] = image
            for side in range(2):
                if x == side * (width_x - 1):
                    edge_ref[side, face, :] = image

    together = 16

    def components(step, carry):
        for index in range(together):
            component(step * together + index)
        return carry

    lax.fori_loop(0, comps // together, components, 0)


def last_kernel(
    dims, row_swaps, part_ref, medium_ref, edge_ref, *refs
):
    comps, width_x, width_y, depth, rows, cols = dims
    corner_refs = refs[:row_swaps]
    image_ref, volume_ref, plane_ref, total_ref, sent = refs[row_swaps + 1 :]
    row_odd = lax.rem(lax.axis_index("row"), 2)
    col_odd = lax.rem(lax.axis_index("col"), 2) == 1
    copies = []
    for side in range(2):
        at_x = side * (width_x - 1)
        plane_ref[side] = edge_ref[side]
        for index in range(row_swaps):
            first = corner_refs[index][pl.ds(0, comps), :]
            second = corner_refs[index][pl.ds(comps, comps), :]
            if side:
                line = jnp.where(col_odd, second, first)
            else:
                line = jnp.where(col_odd, first, second)
            at_y = jnp.where(row_odd == index, width_y - 1, 0)
            weight = 1.0 / 12.0 + medium_ref[pl.ds(at_x * width_y + at_y, 1), :] / 27.0
            here = pl.ds(at_y, comps, stride=width_y)
            plane_ref[side, here, :] = plane_ref[side, here, :] - weight * (
                2.0 * line + side_z(line)
            )
        copies.append(
            pltpu.make_async_copy(
                plane_ref.at[side].reshape(comps, width_y, depth),
                volume_ref.at[:, pl.ds(at_x * width_y, width_y), :],
                sent.at[side],
            )
        )
        copies[-1].start()
    total = jnp.sum(part_ref[...], axis=0)
    half, lanes = total.shape
    total_ref[:half] = total[:, : lanes // 2]
    total_ref[half:] = total[:, lanes // 2 :]
    copies.append(pltpu.make_async_copy(total_ref, image_ref, sent.at[2]))
    copies[-1].start()
    for copy in copies:
        copy.wait()


def swap_pairs(count, swap):
    pairs = []
    for low in range(swap, count - 1, 2):
        pairs += [(low, low + 1), (low + 1, low)]
    return pairs


def on_device(wave_field, medium_term, node_flux, node_cell, block_target, boundary_matrix):
    comps, width_x, width_y, depth = wave_field.shape
    rows, cols = lax.axis_size("row"), lax.axis_size("col")
    dims = (comps, width_x, width_y, depth, rows, cols)
    lines = width_x * width_y
    nodes = node_cell.shape[-1]
    slot_len = nodes // cols
    row_swaps = 1 if rows == 2 else 2
    slab_rows, span = boundary_matrix.shape[1:]
    own_rows = slab_rows // cols
    f32, bf16 = jnp.float32, jnp.bfloat16
    params = pltpu.CompilerParams(vmem_limit_bytes=SMALL)

    chunks, fold = 2, 4
    field = wave_field.reshape(comps * lines, depth)
    cells = node_cell.reshape(1, nodes)
    targets = block_target.reshape(1, cols)
    flux = node_flux.reshape(comps, 1, nodes)
    medium = medium_term.reshape(lines, depth)

    tiles, *faces = pl.pallas_call(
        functools.partial(trace_kernel, dims, row_swaps),
        out_shape=[jax.ShapeDtypeStruct((rows * cols, TILE_ROWS, 2 * comps), bf16)]
        + [jax.ShapeDtypeStruct((comps * width_x, depth), f32)] * row_swaps
        + [jax.ShapeDtypeStruct((comps, width_y, depth), f32)] * 2,
        in_specs=[hbm()] * 3,
        out_specs=[hbm()] * (3 + row_swaps),
        scratch_shapes=[
            pltpu.SMEM((1, cols), jnp.int32),
            pltpu.VMEM((1, nodes), jnp.int32),
            pltpu.VMEM((comps, lines, depth), f32),
            pltpu.VMEM((chunks, lines // fold, comps // chunks, fold * depth), bf16),
            pltpu.VMEM((rows * cols, TILE_ROWS, 2 * comps), bf16),
            pltpu.VMEM((row_swaps, comps * width_x, depth), f32),
            pltpu.SemaphoreType.DMA((chunks + 2,)),
            pltpu.SemaphoreType.DMA((3 + row_swaps,)),
        ],
        compiler_params=pltpu.CompilerParams(vmem_limit_bytes=WHOLE),
        name="traces",
    )(targets, cells, field.reshape(comps, lines, depth))
    col_sides = [
        lax.ppermute(face, "col", swap_pairs(cols, swap)).reshape(comps * width_y, depth)
        for swap, face in enumerate(faces[row_swaps : row_swaps + 2])
    ]
    row_sides = [
        lax.ppermute(face, "row", swap_pairs(rows, swap))
        for swap, face in enumerate(faces[:row_swaps])
    ]
    received = lax.all_to_all(tiles, ("row", "col"), 0, 0, tiled=True)

    if slot_len % 8:
        received = unpack_tiles(received, slot_len, comps)
    shares = pl.pallas_call(
        functools.partial(boundary_kernel, slot_len, own_rows),
        out_shape=jax.ShapeDtypeStruct((cols, own_rows // 2, 2 * comps), f32),
        in_specs=[vmem()] * 4,
        out_specs=vmem(),
        compiler_params=params,
        name="boundary",
    )(received, boundary_matrix[0], boundary_matrix[1], row_sides[0])
    shares = lax.all_to_all(
        shares, "col", 0, 0, tiled=True, axis_index_groups=[root_first(cols)]
    )

    corners = pl.pallas_call(
        functools.partial(corner_kernel, dims),
        out_shape=[jax.ShapeDtypeStruct((2 * comps, depth), f32)] * row_swaps,
        in_specs=[vmem()] * 2,
        out_specs=[vmem()] * row_swaps,
        compiler_params=params,
        name="corners",
    )(*col_sides)
    corner_sides = [
        lax.ppermute(lines_of, "row", swap_pairs(rows, swap))
        for swap, lines_of in enumerate(corners)
    ]

    volume, edges = pl.pallas_call(
        functools.partial(volume_kernel, dims, row_swaps),
        out_shape=[
            jax.ShapeDtypeStruct((comps * lines, depth), f32),
            jax.ShapeDtypeStruct((2, comps * width_y, depth), f32),
        ],
        in_specs=[vmem()] * (6 + row_swaps),
        out_specs=[vmem()] * 2,
        scratch_shapes=[
            pltpu.VMEM((comps * lines // 2, nodes), bf16),
            pltpu.VMEM((comps * lines // 2, 2 * depth), f32),
        ],
        compiler_params=params,
        name="volume",
    )(field, medium, flux, cells, *row_sides, *col_sides)

    boundary_image, volume = pl.pallas_call(
        functools.partial(last_kernel, dims, row_swaps),
        out_shape=[
            jax.ShapeDtypeStruct((own_rows, comps), f32),
            jax.ShapeDtypeStruct((comps, lines, depth), f32),
        ],
        in_specs=[vmem()] * (3 + row_swaps) + [hbm()],
        out_specs=[hbm(), hbm()],
        scratch_shapes=[
            pltpu.VMEM((2, comps * width_y, depth), f32),
            pltpu.VMEM((own_rows, comps), f32),
            pltpu.SemaphoreType.DMA((3,)),
        ],
        input_output_aliases={3 + row_swaps: 1},
        compiler_params=params,
        name="last",
    )(shares, medium, edges, *corner_sides, volume.reshape(comps, lines, depth))
    return (volume.reshape(comps, width_x, width_y, depth), boundary_image)


def solution(mesh):
    in_specs = (
        P(None, "col", "row", None),
        P("col", "row", None),
        P(None, "col", "row", None),
        P("col", "row", None),
        P("col", "row", None),
        P(None, "row", "col"),
    )
    out_specs = (P(None, "col", "row", None), P(("row", "col"), None))
    return jax.shard_map(
        on_device, mesh=mesh, in_specs=in_specs, out_specs=out_specs, check_vma=False
    )
```

```python
import functools

import jax
import jax.numpy as jnp
from jax import lax
from jax.experimental import pallas as pl
from jax.experimental.pallas import tpu as pltpu
from jax.sharding import PartitionSpec as P

TILE_ROWS = 16
SMALL = 8 * 2**20
WHOLE = 64560 * 2**10


def vmem():
    return pl.BlockSpec(memory_space=pltpu.VMEM)


def hbm():
    return pl.BlockSpec(memory_space=pltpu.HBM)


def folded_hot(cells, depth, lines, fold):
    few = lines // fold
    line = jnp.right_shift(cells, depth.bit_length() - 1)
    own = jnp.bitwise_and(line, few - 1)
    key = jnp.right_shift(line, few.bit_length() - 1) * depth + jnp.bitwise_and(cells, depth - 1)
    at = lax.broadcasted_iota(jnp.int32, (fold * depth, cells.shape[1]), 0)
    return jnp.where(at == key, 1.0, 0.0).astype(jnp.bfloat16), own


def root_first(count):
    root = count * 11 // 16
    return [root] + [index for index in range(count) if index != root]


def trace_kernel(dims, row_swaps, target_hbm, cell_hbm, field_hbm, tile_hbm, *rest):
    comps, width_x, width_y, depth, rows, cols = dims
    row_faces, col_faces = rest[:row_swaps], rest[row_swaps : row_swaps + 2]
    target_ref, cell_ref, field_ref, lhs_ref, tile_ref, side_ref, arrived, left_sem = rest[
        row_swaps + 2 :
    ]
    lines = width_x * width_y
    nodes = cell_ref.shape[1]
    slot_len = nodes // cols
    chunks, few = lhs_ref.shape[:2]
    fold = lines // few
    span = comps // chunks
    copies = [pltpu.make_async_copy(cell_hbm, cell_ref, arrived.at[chunks])]
    for chunk in range(chunks):
        part = pl.ds(chunk * span, span)
        copies.append(
            pltpu.make_async_copy(field_hbm.at[part], field_ref.at[part], arrived.at[chunk])
        )
    copies.append(pltpu.make_async_copy(target_hbm, target_ref, arrived.at[chunks + 1]))
    for copy in copies:
        copy.start()
    sent = []
    copies[0].wait()
    hot, own = folded_hot(cell_ref[...], depth, lines, fold)
    own = jnp.broadcast_to(own, (8, nodes))
    flat = field_ref.reshape(comps * lines, depth)
    found = []
    for chunk in range(chunks):
        copies[1 + chunk].wait()
        for line in range(lines):
            lhs_ref[chunk, line % few, :, pl.ds(line // few * depth, depth)] = flat[
                pl.ds(chunk * span * lines + line, span, stride=lines), :
            ].astype(jnp.bfloat16)
        total = jnp.zeros((span // 8, 8, nodes), jnp.float32)
        group = min(4, few)
        for first in range(0, few, group):
            block = jnp.dot(
                lhs_ref[chunk, first : first + group].reshape(group * span, fold * depth),
                hot,
                preferred_element_type=jnp.float32,
            ).reshape(group, span // 8, 8, nodes)
            for line in range(group):
                total = jnp.where((own == first + line)[None], block[line], total)
        found.append(total.reshape(span, nodes))
    col_odd = lax.rem(lax.axis_index("col"), 2)
    for swap, face_ref in enumerate(col_faces):
        layer = jnp.where(col_odd == swap, width_x - 1, 0)
        start = pl.multiple_of(layer * width_y, width_y)
        sent.append(
            pltpu.make_async_copy(
                field_ref.at[:, pl.ds(start, width_y), :], face_ref, left_sem.at[swap]
            )
        )
        sent[-1].start()
    row_odd = lax.rem(lax.axis_index("row"), 2)
    for swap, face_ref in enumerate(row_faces):
        layer = jnp.where(row_odd == swap, width_y - 1, 0)
        side_ref[swap] = flat[pl.ds(layer, comps * width_x, stride=width_y), :]
        sent.append(pltpu.make_async_copy(side_ref.at[swap], face_ref, left_sem.at[2 + swap]))
        sent[-1].start()
    by_node = jnp.concatenate(found, axis=0).T
    copies[-1].wait()
    left_len = min(slot_len, TILE_ROWS)
    for slot in range(cols):
        piece = by_node[slot * slot_len : (slot + 1) * slot_len]
        left = piece[:left_len]
        right = piece[left_len:]
        if left_len < TILE_ROWS:
            left = jnp.concatenate(
                [left, jnp.zeros((TILE_ROWS - left_len, comps), jnp.float32)], axis=0
            )
        gap = TILE_ROWS - (slot_len - left_len)
        if slot_len == left_len:
            right = jnp.zeros((TILE_ROWS, comps), jnp.float32)
        elif gap:
            right = jnp.concatenate([right, jnp.zeros((gap, comps), jnp.float32)], axis=0)
        tile = jnp.concatenate([left, right], axis=1).astype(jnp.bfloat16)
        for row in range(rows):
            tile_ref[row * cols + target_ref[0, slot]] = tile
    sent.append(pltpu.make_async_copy(tile_ref, tile_hbm, left_sem.at[2 + row_swaps]))
    sent[-1].start()
    for copy in sent:
        copy.wait()


def corner_kernel(dims, first_ref, second_ref, *out_refs):
    comps, width_x, width_y = dims[:3]
    odd = lax.rem(lax.axis_index("row"), 2)
    for swap, out_ref in enumerate(out_refs):
        layer = jnp.where(odd == swap, width_y - 1, 0)
        for index, ref in enumerate((first_ref, second_ref)):
            out_ref[pl.ds(index * comps, comps), :] = ref[
                pl.ds(layer, comps, stride=width_y), :
            ].astype(out_ref.dtype)


def unpack_tiles(tiles, slot_len, comps):
    left_len = min(slot_len, TILE_ROWS)
    parts = [tiles[:, :left_len, :comps]]
    if slot_len > left_len:
        parts.append(tiles[:, : slot_len - left_len, comps:])
    both = jnp.concatenate(parts, axis=1) if len(parts) > 1 else parts[0]
    return both.reshape(tiles.shape[0] * slot_len, comps)


def boundary_kernel(slot_len, own_rows, trace_ref, real_ref, imag_ref, row_ref, out_ref):
    if len(trace_ref.shape) == 3:
        traces = unpack_tiles(
            trace_ref[...].astype(jnp.float32), slot_len, trace_ref.shape[2] // 2
        )
    else:
        traces = trace_ref[...].astype(jnp.float32)
    comps = traces.shape[1]
    angles = comps // 2
    turned = jnp.concatenate([-traces[:, angles:], traces[:, :angles]], axis=1)
    image = jnp.dot(
        real_ref[...], traces.astype(jnp.bfloat16), preferred_element_type=jnp.float32
    ) + jnp.dot(imag_ref[...], turned.astype(jnp.bfloat16), preferred_element_type=jnp.float32)
    image = image.reshape(image.shape[0] // own_rows, own_rows, comps)
    half = own_rows // 2
    packed = jnp.concatenate([image[:, :half], image[:, half:]], axis=2).astype(out_ref.dtype)
    for place, col in enumerate(root_first(packed.shape[0])):
        out_ref[place] = packed[col]


def shifted_z(values, step):
    rows, depth = values.shape
    at_z = lax.broadcasted_iota(jnp.int32, (rows, depth), 1)
    outside = at_z == (0 if step == 1 else depth - 1)
    return jnp.where(outside, 0.0, pltpu.roll(values, step % depth, 1))


def side_z(values):
    return shifted_z(values, 1) + shifted_z(values, -1)


def volume_kernel(dims, row_swaps, *refs):
    comps, width_x, width_y, depth, rows, cols = dims
    field_ref, medium_ref, flux_ref, cell_ref = refs[:4]
    row_refs = refs[4 : 4 + row_swaps]
    first_ref, second_ref = refs[4 + row_swaps : 6 + row_swaps]
    out_ref, edge_ref, lhs_ref, taken_ref = refs[6 + row_swaps :]
    lines = width_x * width_y
    nodes = cell_ref.shape[1]
    fold = 2
    few = lines // fold
    hot, own = folded_hot(cell_ref[...], depth, lines, fold)
    at_line = lax.broadcasted_iota(jnp.int32, (few, nodes), 0)
    line_hot = jnp.where(at_line == own, 1.0, 0.0)
    for comp in range(comps):
        lhs_ref[pl.ds(comp * few, few), :] = (
            line_hot * jnp.broadcast_to(flux_ref[comp], (few, nodes))
        ).astype(jnp.bfloat16)
    taken_ref[...] = lax.dot_general(
        lhs_ref[...], hot, (((1,), (1,)), ((), ())), preferred_element_type=jnp.float32
    )

    row_odd = lax.rem(lax.axis_index("row"), 2) == 1
    col_odd = lax.rem(lax.axis_index("col"), 2) == 1
    shape = (width_y, depth)
    at_y = lax.broadcasted_iota(jnp.int32, shape, 0)
    low_y, high_y = at_y == 0, at_y == width_y - 1
    weight = [1.0 / 12.0 + medium_ref[pl.ds(x * width_y, width_y), :] / 27.0 for x in range(width_x)]
    from_first = jnp.logical_or(
        jnp.logical_and(high_y, jnp.logical_not(row_odd)), jnp.logical_and(low_y, row_odd)
    )

    def side_y(values, ends):
        lower = jnp.where(low_y, ends, pltpu.roll(values, 1, 0))
        upper = jnp.where(high_y, ends, pltpu.roll(values, width_y - 1, 0))
        return lower + upper

    def wide(ref, index):
        return jnp.broadcast_to(ref[pl.ds(index, 1), :], shape)

    def component(comp):
        base = comp * lines
        planes = [
            field_ref[pl.ds(base + x * width_y, width_y), :]
            for x in range(width_x)
        ]
        face = pl.ds(comp * width_y, width_y)
        first, second = first_ref[face, :], second_ref[face, :]
        planes = (
            [jnp.where(col_odd, first, second)] + planes + [jnp.where(col_odd, second, first)]
        )
        ends = []
        for x in range(width_x):
            line = [wide(row_ref, comp * width_x + x) for row_ref in row_refs]
            ends.append(jnp.where(from_first, line[0], line[1] if row_swaps > 1 else 0.0))
        none = jnp.zeros(shape, jnp.float32)
        ends = [none] + ends + [none]
        for x in range(width_x):
            centre = planes[x + 1]
            sides = planes[x] + planes[x + 2]
            over_x = 2.0 * centre + sides
            ends_x = 2.0 * ends[x + 1] + (ends[x] + ends[x + 2])
            over_xy = 2.0 * over_x + side_y(over_x, ends_x)
            over_xyz = 2.0 * over_xy + side_z(over_xy)
            near = sides + side_y(centre, ends[x + 1]) + side_z(centre)
            here = pl.ds(base + x * width_y, width_y)
            image = (
                (10.0 / 3.0) * centre
                + (1.0 / 3.0) * near
                - weight[x] * over_xyz
                - taken_ref[
                    pl.ds(
                        pl.multiple_of(comp * few + x * width_y % few, width_y), width_y
                    ),
                    pl.ds(x * width_y // few * depth, depth),
                ]
            )
            out_ref[here, :] = image
            for side in range(2):
                if x == side * (width_x - 1):
                    edge_ref[side, face, :] = image

    for comp in range(comps):
        component(comp)


def last_kernel(
    dims, row_swaps, part_ref, medium_ref, edge_ref, *refs
):
    comps, width_x, width_y, depth, rows, cols = dims
    corner_refs = refs[:row_swaps]
    image_ref, volume_ref, plane_ref, total_ref, sent = refs[row_swaps + 1 :]
    row_odd = lax.rem(lax.axis_index("row"), 2)
    col_odd = lax.rem(lax.axis_index("col"), 2) == 1
    total = jnp.sum(part_ref[...].astype(jnp.float32), axis=0)
    half, lanes = total.shape
    total_ref[:half] = total[:, : lanes // 2]
    total_ref[half:] = total[:, lanes // 2 :]
    copies = [pltpu.make_async_copy(total_ref, image_ref, sent.at[2])]
    copies[-1].start()
    for side in range(2):
        at_x = side * (width_x - 1)
        plane_ref[side] = edge_ref[side]
        for index in range(row_swaps):
            first = corner_refs[index][pl.ds(0, comps), :].astype(jnp.float32)
            second = corner_refs[index][pl.ds(comps, comps), :].astype(jnp.float32)
            if side:
                line = jnp.where(col_odd, second, first)
            else:
                line = jnp.where(col_odd, first, second)
            at_y = jnp.where(row_odd == index, width_y - 1, 0)
            weight = 1.0 / 12.0 + medium_ref[pl.ds(at_x * width_y + at_y, 1), :] / 27.0
            here = pl.ds(at_y, comps, stride=width_y)
            plane_ref[side, here, :] = plane_ref[side, here, :] - weight * (
                2.0 * line + side_z(line)
            )
        copies.append(
            pltpu.make_async_copy(
                plane_ref.at[side].reshape(comps, width_y, depth),
                volume_ref.at[:, pl.ds(at_x * width_y, width_y), :],
                sent.at[side],
            )
        )
        copies[-1].start()
    for copy in copies:
        copy.wait()


def swap_pairs(count, swap):
    pairs = []
    for low in range(swap, count - 1, 2):
        pairs += [(low, low + 1), (low + 1, low)]
    return pairs


def on_device(wave_field, medium_term, node_flux, node_cell, block_target, boundary_matrix):
    comps, width_x, width_y, depth = wave_field.shape
    rows, cols = lax.axis_size("row"), lax.axis_size("col")
    dims = (comps, width_x, width_y, depth, rows, cols)
    lines = width_x * width_y
    nodes = node_cell.shape[-1]
    slot_len = nodes // cols
    row_swaps = 1 if rows == 2 else 2
    slab_rows, span = boundary_matrix.shape[1:]
    own_rows = slab_rows // cols
    f32, bf16 = jnp.float32, jnp.bfloat16
    params = pltpu.CompilerParams(vmem_limit_bytes=SMALL)

    chunks, fold = 2, 4
    field = wave_field.reshape(comps * lines, depth)
    cells = node_cell.reshape(1, nodes)
    targets = block_target.reshape(1, cols)
    flux = node_flux.reshape(comps, 1, nodes)
    medium = medium_term.reshape(lines, depth)

    tiles, *faces = pl.pallas_call(
        functools.partial(trace_kernel, dims, row_swaps),
        out_shape=[jax.ShapeDtypeStruct((rows * cols, TILE_ROWS, 2 * comps), bf16)]
        + [jax.ShapeDtypeStruct((comps * width_x, depth), f32)] * row_swaps
        + [jax.ShapeDtypeStruct((comps, width_y, depth), f32)] * 2,
        in_specs=[hbm()] * 3,
        out_specs=[hbm()] * (3 + row_swaps),
        scratch_shapes=[
            pltpu.SMEM((1, cols), jnp.int32),
            pltpu.VMEM((1, nodes), jnp.int32),
            pltpu.VMEM((comps, lines, depth), f32),
            pltpu.VMEM((chunks, lines // fold, comps // chunks, fold * depth), bf16),
            pltpu.VMEM((rows * cols, TILE_ROWS, 2 * comps), bf16),
            pltpu.VMEM((row_swaps, comps * width_x, depth), f32),
            pltpu.SemaphoreType.DMA((chunks + 2,)),
            pltpu.SemaphoreType.DMA((3 + row_swaps,)),
        ],
        compiler_params=pltpu.CompilerParams(vmem_limit_bytes=WHOLE),
        name="traces",
    )(targets, cells, field.reshape(comps, lines, depth))
    col_sides = [
        lax.ppermute(face, "col", swap_pairs(cols, swap)).reshape(comps * width_y, depth)
        for swap, face in enumerate(faces[row_swaps : row_swaps + 2])
    ]
    row_sides = [
        lax.ppermute(face, "row", swap_pairs(rows, swap))
        for swap, face in enumerate(faces[:row_swaps])
    ]
    received = lax.all_to_all(tiles, ("row", "col"), 0, 0, tiled=True)

    if slot_len % 8:
        received = unpack_tiles(received, slot_len, comps)
    shares = pl.pallas_call(
        functools.partial(boundary_kernel, slot_len, own_rows),
        out_shape=jax.ShapeDtypeStruct((cols, own_rows // 2, 2 * comps), bf16),
        in_specs=[vmem()] * 4,
        out_specs=vmem(),
        compiler_params=params,
        name="boundary",
    )(received, boundary_matrix[0], boundary_matrix[1], row_sides[0])
    shares = lax.all_to_all(
        shares, "col", 0, 0, tiled=True, axis_index_groups=[root_first(cols)]
    )

    corners = pl.pallas_call(
        functools.partial(corner_kernel, dims),
        out_shape=[jax.ShapeDtypeStruct((2 * comps, depth), bf16)] * row_swaps,
        in_specs=[vmem()] * 2,
        out_specs=[vmem()] * row_swaps,
        compiler_params=params,
        name="corners",
    )(*col_sides)
    corner_sides = [
        lax.ppermute(lines_of, "row", swap_pairs(rows, swap))
        for swap, lines_of in enumerate(corners)
    ]

    volume, edges = pl.pallas_call(
        functools.partial(volume_kernel, dims, row_swaps),
        out_shape=[
            jax.ShapeDtypeStruct((comps * lines, depth), f32),
            jax.ShapeDtypeStruct((2, comps * width_y, depth), f32),
        ],
        in_specs=[vmem()] * (6 + row_swaps),
        out_specs=[vmem()] * 2,
        scratch_shapes=[
            pltpu.VMEM((comps * lines // 2, nodes), bf16),
            pltpu.VMEM((comps * lines // 2, 2 * depth), f32),
        ],
        compiler_params=params,
        name="volume",
    )(field, medium, flux, cells, *row_sides, *col_sides)

    boundary_image, volume = pl.pallas_call(
        functools.partial(last_kernel, dims, row_swaps),
        out_shape=[
            jax.ShapeDtypeStruct((own_rows, comps), f32),
            jax.ShapeDtypeStruct((comps, lines, depth), f32),
        ],
        in_specs=[vmem()] * (3 + row_swaps) + [hbm()],
        out_specs=[hbm(), hbm()],
        scratch_shapes=[
            pltpu.VMEM((2, comps * width_y, depth), f32),
            pltpu.VMEM((own_rows, comps), f32),
            pltpu.SemaphoreType.DMA((3,)),
        ],
        input_output_aliases={3 + row_swaps: 1},
        compiler_params=params,
        name="last",
    )(shares, medium, edges, *corner_sides, volume.reshape(comps, lines, depth))
    return (volume.reshape(comps, width_x, width_y, depth), boundary_image)


def solution(mesh):
    in_specs = (
        P(None, "col", "row", None),
        P("col", "row", None),
        P(None, "col", "row", None),
        P("col", "row", None),
        P("col", "row", None),
        P(None, "row", "col"),
    )
    out_specs = (P(None, "col", "row", None), P(("row", "col"), None))
    return jax.shard_map(
        on_device, mesh=mesh, in_specs=in_specs, out_specs=out_specs, check_vma=False
    )
```

```python
import functools

import jax
import jax.numpy as jnp
from jax import lax
from jax.experimental import pallas as pl
from jax.experimental.pallas import tpu as pltpu
from jax.sharding import PartitionSpec as P

SMALL = 8 * 2**20
WHOLE = 64560 * 2**10


def vmem():
    return pl.BlockSpec(memory_space=pltpu.VMEM)


def hbm():
    return pl.BlockSpec(memory_space=pltpu.HBM)


def folded_hot(cells, depth, lines, fold):
    few = lines // fold
    line = jnp.right_shift(cells, depth.bit_length() - 1)
    own = jnp.bitwise_and(line, few - 1)
    key = jnp.right_shift(line, few.bit_length() - 1) * depth + jnp.bitwise_and(cells, depth - 1)
    at = lax.broadcasted_iota(jnp.int32, (fold * depth, cells.shape[1]), 0)
    return jnp.where(at == key, 1.0, 0.0).astype(jnp.bfloat16), own


def root_first(count):
    root = count * 9 // 16
    return [root] + [index for index in range(count) if index != root]


def tile_shape(slot_len, comps):
    groups = 3 if slot_len % 6 == 0 else 1
    return slot_len // (2 * groups), groups


def trace_kernel(dims, row_swaps, target_hbm, cell_hbm, field_hbm, tile_hbm, *rest):
    comps, width_x, width_y, depth, rows, cols = dims
    row_faces, col_faces = rest[:row_swaps], rest[row_swaps : row_swaps + 2]
    target_ref, cell_ref, field_ref, lhs_ref, tile_ref, side_ref, arrived, left_sem = rest[
        row_swaps + 2 :
    ]
    lines = width_x * width_y
    nodes = cell_ref.shape[1]
    slot_len = nodes // cols
    chunks, few = lhs_ref.shape[:2]
    fold = lines // few
    span = comps // chunks
    copies = [pltpu.make_async_copy(cell_hbm, cell_ref, arrived.at[chunks])]
    for chunk in range(chunks):
        part = pl.ds(chunk * span, span)
        copies.append(
            pltpu.make_async_copy(field_hbm.at[part], field_ref.at[part], arrived.at[chunk])
        )
    copies.append(pltpu.make_async_copy(target_hbm, target_ref, arrived.at[chunks + 1]))
    for copy in copies:
        copy.start()
    sent = []
    copies[0].wait()
    hot, own = folded_hot(cell_ref[...], depth, lines, fold)
    own = jnp.broadcast_to(own, (8, nodes))
    flat = field_ref.reshape(comps * lines, depth)
    found = []
    for chunk in range(chunks):
        copies[1 + chunk].wait()
        for line in range(lines):
            lhs_ref[chunk, line % few, :, pl.ds(line // few * depth, depth)] = flat[
                pl.ds(chunk * span * lines + line, span, stride=lines), :
            ].astype(jnp.bfloat16)
        total = jnp.zeros((span // 8, 8, nodes), jnp.float32)
        group = min(4, few)
        for first in range(0, few, group):
            block = jnp.dot(
                lhs_ref[chunk, first : first + group].reshape(group * span, fold * depth),
                hot,
                preferred_element_type=jnp.float32,
            ).reshape(group, span // 8, 8, nodes)
            for line in range(group):
                total = jnp.where((own == first + line)[None], block[line], total)
        found.append(total.reshape(span, nodes))
    col_odd = lax.rem(lax.axis_index("col"), 2)
    for swap, face_ref in enumerate(col_faces):
        layer = jnp.where(col_odd == swap, width_x - 1, 0)
        start = pl.multiple_of(layer * width_y, width_y)
        sent.append(
            pltpu.make_async_copy(
                field_ref.at[:, pl.ds(start, width_y), :], face_ref, left_sem.at[swap]
            )
        )
        sent[-1].start()
    row_odd = lax.rem(lax.axis_index("row"), 2)
    for swap, face_ref in enumerate(row_faces):
        layer = jnp.where(row_odd == swap, width_y - 1, 0)
        side_ref[swap] = flat[pl.ds(layer, comps * width_x, stride=width_y), :].astype(jnp.bfloat16)
        sent.append(pltpu.make_async_copy(side_ref.at[swap], face_ref, left_sem.at[2 + swap]))
        sent[-1].start()
    by_node = jnp.concatenate(found, axis=0).T
    copies[-1].wait()
    tile_rows, groups = tile_shape(slot_len, comps)
    for slot in range(cols):
        pieces = []
        for group in range(2 * groups):
            start = slot * slot_len + group * tile_rows
            pieces.append(by_node[start : start + tile_rows])
        tile = jnp.concatenate(pieces, axis=1).astype(jnp.bfloat16)
        for row in range(rows):
            tile_ref[row * cols + target_ref[0, slot]] = tile
    sent.append(pltpu.make_async_copy(tile_ref, tile_hbm, left_sem.at[2 + row_swaps]))
    sent[-1].start()
    for copy in sent:
        copy.wait()


def corner_kernel(dims, first_ref, second_ref, *out_refs):
    comps, width_x, width_y = dims[:3]
    odd = lax.rem(lax.axis_index("row"), 2)
    for swap, out_ref in enumerate(out_refs):
        layer = jnp.where(odd == swap, width_y - 1, 0)
        for index, ref in enumerate((first_ref, second_ref)):
            out_ref[pl.ds(index * comps, comps), :] = ref[
                pl.ds(layer, comps, stride=width_y), :
            ].astype(out_ref.dtype)


def unpack_tiles(tiles, comps):
    groups = tiles.shape[2] // comps
    parts = [tiles[:, :, group * comps : (group + 1) * comps] for group in range(groups)]
    return jnp.concatenate(parts, axis=1).reshape(-1, comps)


def boundary_kernel(slot_len, own_rows, trace_ref, real_ref, imag_ref, row_ref, out_ref):
    if len(trace_ref.shape) == 3:
        traces = unpack_tiles(trace_ref[...].astype(jnp.float32), 2 * out_ref.shape[2] // 4)
    else:
        traces = trace_ref[...].astype(jnp.float32)
    comps = traces.shape[1]
    angles = comps // 2
    turned = jnp.concatenate([-traces[:, angles:], traces[:, :angles]], axis=1)
    image = jnp.dot(
        real_ref[...], traces.astype(jnp.bfloat16), preferred_element_type=jnp.float32
    ) + jnp.dot(imag_ref[...], turned.astype(jnp.bfloat16), preferred_element_type=jnp.float32)
    image = image.reshape(image.shape[0] // own_rows, own_rows, comps)
    half = own_rows // 2
    packed = jnp.concatenate([image[:, :half], image[:, half:]], axis=2).astype(out_ref.dtype)
    for place, col in enumerate(root_first(packed.shape[0])):
        out_ref[place] = packed[col]


def shifted_z(values, step):
    rows, depth = values.shape
    at_z = lax.broadcasted_iota(jnp.int32, (rows, depth), 1)
    outside = at_z == (0 if step == 1 else depth - 1)
    return jnp.where(outside, 0.0, pltpu.roll(values, step % depth, 1))


def side_z(values):
    return shifted_z(values, 1) + shifted_z(values, -1)


def volume_kernel(dims, row_swaps, *refs):
    comps, width_x, width_y, depth, rows, cols = dims
    field_ref, medium_ref, flux_ref, cell_ref = refs[:4]
    row_refs = refs[4 : 4 + row_swaps]
    first_ref, second_ref = refs[4 + row_swaps : 6 + row_swaps]
    out_hbm, edge_ref, lhs_ref, taken_ref, out_ref, side_ref, sent = refs[6 + row_swaps :]
    for index, row_ref in enumerate(row_refs):
        side_ref[index] = row_ref[...].astype(jnp.float32)
    lines = width_x * width_y
    nodes = cell_ref.shape[1]
    fold = 2
    few = lines // fold
    hot, own = folded_hot(cell_ref[...], depth, lines, fold)
    at_line = lax.broadcasted_iota(jnp.int32, (few, nodes), 0)
    line_hot = jnp.where(at_line == own, 1.0, 0.0)
    for comp in range(comps):
        lhs_ref[pl.ds(comp * few, few), :] = (
            line_hot * jnp.broadcast_to(flux_ref[comp], (few, nodes))
        ).astype(jnp.bfloat16)
    taken_ref[...] = lax.dot_general(
        lhs_ref[...], hot, (((1,), (1,)), ((), ())), preferred_element_type=jnp.float32
    )

    row_odd = lax.rem(lax.axis_index("row"), 2) == 1
    col_odd = lax.rem(lax.axis_index("col"), 2) == 1
    shape = (width_y, depth)
    at_y = lax.broadcasted_iota(jnp.int32, shape, 0)
    low_y, high_y = at_y == 0, at_y == width_y - 1
    weight = [1.0 / 12.0 + medium_ref[pl.ds(x * width_y, width_y), :] / 27.0 for x in range(width_x)]
    from_first = jnp.logical_or(
        jnp.logical_and(high_y, jnp.logical_not(row_odd)), jnp.logical_and(low_y, row_odd)
    )

    def side_y(values, ends):
        lower = jnp.where(low_y, ends, pltpu.roll(values, 1, 0))
        upper = jnp.where(high_y, ends, pltpu.roll(values, width_y - 1, 0))
        return lower + upper

    def wide(ref, index):
        return jnp.broadcast_to(ref[pl.ds(index, 1), :], shape)

    def component(comp):
        base = comp * lines
        planes = [
            field_ref[pl.ds(base + x * width_y, width_y), :]
            for x in range(width_x)
        ]
        face = pl.ds(comp * width_y, width_y)
        first, second = first_ref[face, :], second_ref[face, :]
        planes = (
            [jnp.where(col_odd, first, second)] + planes + [jnp.where(col_odd, second, first)]
        )
        ends = []
        for x in range(width_x):
            line = [wide(side_ref.at[index], comp * width_x + x) for index in range(row_swaps)]
            ends.append(jnp.where(from_first, line[0], line[1] if row_swaps > 1 else 0.0))
        none = jnp.zeros(shape, jnp.float32)
        ends = [none] + ends + [none]
        for x in range(width_x):
            centre = planes[x + 1]
            sides = planes[x] + planes[x + 2]
            over_x = 2.0 * centre + sides
            ends_x = 2.0 * ends[x + 1] + (ends[x] + ends[x + 2])
            over_xy = 2.0 * over_x + side_y(over_x, ends_x)
            over_xyz = 2.0 * over_xy + side_z(over_xy)
            near = sides + side_y(centre, ends[x + 1]) + side_z(centre)
            here = pl.ds(base + x * width_y, width_y)
            image = (
                (10.0 / 3.0) * centre
                + (1.0 / 3.0) * near
                - weight[x] * over_xyz
                - taken_ref[
                    pl.ds(
                        pl.multiple_of(comp * few + x * width_y % few, width_y), width_y
                    ),
                    pl.ds(x * width_y // few * depth, depth),
                ]
            )
            out_ref[here, :] = image
            for side in range(2):
                if x == side * (width_x - 1):
                    edge_ref[side, face, :] = image

    steps = sent.shape[0]
    together = comps // steps
    copies = []
    for step in range(steps):
        for comp in range(step * together, (step + 1) * together):
            component(comp)
        here = pl.ds(step * together * lines, together * lines)
        copies.append(
            pltpu.make_async_copy(out_ref.at[here, :], out_hbm.at[here, :], sent.at[step])
        )
        copies[-1].start()
    for copy in copies:
        copy.wait()


def last_kernel(
    dims, row_swaps, part_ref, medium_ref, edge_ref, *refs
):
    comps, width_x, width_y, depth, rows, cols = dims
    corner_refs = refs[:row_swaps]
    image_ref, volume_ref, plane_ref, total_ref, sent = refs[row_swaps + 1 :]
    row_odd = lax.rem(lax.axis_index("row"), 2)
    col_odd = lax.rem(lax.axis_index("col"), 2) == 1
    total = jnp.sum(part_ref[...].astype(jnp.float32), axis=0)
    half, lanes = total.shape
    total_ref[:half] = total[:, : lanes // 2]
    total_ref[half:] = total[:, lanes // 2 :]
    copies = [pltpu.make_async_copy(total_ref, image_ref, sent.at[2])]
    copies[-1].start()
    for side in range(2):
        at_x = side * (width_x - 1)
        plane_ref[side] = edge_ref[side]
        for index in range(row_swaps):
            first = corner_refs[index][pl.ds(0, comps), :].astype(jnp.float32)
            second = corner_refs[index][pl.ds(comps, comps), :].astype(jnp.float32)
            if side:
                line = jnp.where(col_odd, second, first)
            else:
                line = jnp.where(col_odd, first, second)
            at_y = jnp.where(row_odd == index, width_y - 1, 0)
            weight = 1.0 / 12.0 + medium_ref[pl.ds(at_x * width_y + at_y, 1), :] / 27.0
            here = pl.ds(at_y, comps, stride=width_y)
            plane_ref[side, here, :] = plane_ref[side, here, :] - weight * (
                2.0 * line + side_z(line)
            )
        copies.append(
            pltpu.make_async_copy(
                plane_ref.at[side].reshape(comps, width_y, depth),
                volume_ref.at[:, pl.ds(at_x * width_y, width_y), :],
                sent.at[side],
            )
        )
        copies[-1].start()
    for copy in copies:
        copy.wait()


def swap_pairs(count, swap):
    pairs = []
    for low in range(swap, count - 1, 2):
        pairs += [(low, low + 1), (low + 1, low)]
    return pairs


def on_device(wave_field, medium_term, node_flux, node_cell, block_target, boundary_matrix):
    comps, width_x, width_y, depth = wave_field.shape
    rows, cols = lax.axis_size("row"), lax.axis_size("col")
    dims = (comps, width_x, width_y, depth, rows, cols)
    lines = width_x * width_y
    nodes = node_cell.shape[-1]
    slot_len = nodes // cols
    row_swaps = 1 if rows == 2 else 2
    slab_rows, span = boundary_matrix.shape[1:]
    own_rows = slab_rows // cols
    f32, bf16 = jnp.float32, jnp.bfloat16
    params = pltpu.CompilerParams(vmem_limit_bytes=SMALL)

    chunks, fold = 2, 4
    tile_rows, groups = tile_shape(slot_len, comps)
    tile_dims = (tile_rows, 2 * groups * comps)
    field = wave_field.reshape(comps * lines, depth)
    cells = node_cell.reshape(1, nodes)
    targets = block_target.reshape(1, cols)
    flux = node_flux.reshape(comps, 1, nodes)
    medium = medium_term.reshape(lines, depth)

    tiles, *faces = pl.pallas_call(
        functools.partial(trace_kernel, dims, row_swaps),
        out_shape=[jax.ShapeDtypeStruct((rows * cols,) + tile_dims, bf16)]
        + [jax.ShapeDtypeStruct((comps * width_x, depth), bf16)] * row_swaps
        + [jax.ShapeDtypeStruct((comps, width_y, depth), f32)] * 2,
        in_specs=[hbm()] * 3,
        out_specs=[hbm()] * (3 + row_swaps),
        scratch_shapes=[
            pltpu.SMEM((1, cols), jnp.int32),
            pltpu.VMEM((1, nodes), jnp.int32),
            pltpu.VMEM((comps, lines, depth), f32),
            pltpu.VMEM((chunks, lines // fold, comps // chunks, fold * depth), bf16),
            pltpu.VMEM((rows * cols,) + tile_dims, bf16),
            pltpu.VMEM((row_swaps, comps * width_x, depth), bf16),
            pltpu.SemaphoreType.DMA((chunks + 2,)),
            pltpu.SemaphoreType.DMA((3 + row_swaps,)),
        ],
        compiler_params=pltpu.CompilerParams(vmem_limit_bytes=WHOLE),
        name="traces",
    )(targets, cells, field.reshape(comps, lines, depth))
    col_sides = [
        lax.ppermute(face, "col", swap_pairs(cols, swap)).reshape(comps * width_y, depth)
        for swap, face in enumerate(faces[row_swaps : row_swaps + 2])
    ]
    row_sides = [
        lax.ppermute(face, "row", swap_pairs(rows, swap))
        for swap, face in enumerate(faces[:row_swaps])
    ]
    received = lax.all_to_all(tiles, ("row", "col"), 0, 0, tiled=True)

    if slot_len % 8:
        received = unpack_tiles(received, comps)
    shares = pl.pallas_call(
        functools.partial(boundary_kernel, slot_len, own_rows),
        out_shape=jax.ShapeDtypeStruct((cols, own_rows // 2, 2 * comps), bf16),
        in_specs=[vmem()] * 4,
        out_specs=vmem(),
        compiler_params=params,
        name="boundary",
    )(received, boundary_matrix[0], boundary_matrix[1], row_sides[0])
    shares = lax.all_to_all(
        shares, "col", 0, 0, tiled=True, axis_index_groups=[root_first(cols)]
    )

    corners = pl.pallas_call(
        functools.partial(corner_kernel, dims),
        out_shape=[jax.ShapeDtypeStruct((2 * comps, depth), bf16)] * row_swaps,
        in_specs=[vmem()] * 2,
        out_specs=[vmem()] * row_swaps,
        compiler_params=params,
        name="corners",
    )(*col_sides)
    corner_sides = [
        lax.ppermute(lines_of, "row", swap_pairs(rows, swap))
        for swap, lines_of in enumerate(corners)
    ]

    volume, edges = pl.pallas_call(
        functools.partial(volume_kernel, dims, row_swaps),
        out_shape=[
            jax.ShapeDtypeStruct((comps * lines, depth), f32),
            jax.ShapeDtypeStruct((2, comps * width_y, depth), f32),
        ],
        in_specs=[vmem()] * (6 + row_swaps),
        out_specs=[hbm(), vmem()],
        scratch_shapes=[
            pltpu.VMEM((comps * lines // 2, nodes), bf16),
            pltpu.VMEM((comps * lines // 2, 2 * depth), f32),
            pltpu.VMEM((comps * lines, depth), f32),
            pltpu.VMEM((row_swaps, comps * width_x, depth), f32),
            pltpu.SemaphoreType.DMA((8,)),
        ],
        compiler_params=params,
        name="volume",
    )(field, medium, flux, cells, *row_sides, *col_sides)

    boundary_image, volume = pl.pallas_call(
        functools.partial(last_kernel, dims, row_swaps),
        out_shape=[
            jax.ShapeDtypeStruct((own_rows, comps), f32),
            jax.ShapeDtypeStruct((comps, lines, depth), f32),
        ],
        in_specs=[vmem()] * (3 + row_swaps) + [hbm()],
        out_specs=[hbm(), hbm()],
        scratch_shapes=[
            pltpu.VMEM((2, comps * width_y, depth), f32),
            pltpu.VMEM((own_rows, comps), f32),
            pltpu.SemaphoreType.DMA((3,)),
        ],
        input_output_aliases={3 + row_swaps: 1},
        compiler_params=params,
        name="last",
    )(shares, medium, edges, *corner_sides, volume.reshape(comps, lines, depth))
    return (volume.reshape(comps, width_x, width_y, depth), boundary_image)


def solution(mesh):
    in_specs = (
        P(None, "col", "row", None),
        P("col", "row", None),
        P(None, "col", "row", None),
        P("col", "row", None),
        P("col", "row", None),
        P(None, "row", "col"),
    )
    out_specs = (P(None, "col", "row", None), P(("row", "col"), None))
    return jax.shard_map(
        on_device, mesh=mesh, in_specs=in_specs, out_specs=out_specs, check_vma=False
    )
```

```python
import functools

import jax
import jax.numpy as jnp
from jax import lax
from jax.experimental import pallas as pl
from jax.experimental.pallas import tpu as pltpu
from jax.sharding import PartitionSpec as P

TILE_ROWS = 16
SMALL = 8 * 2**20
WHOLE = 64560 * 2**10


def vmem():
    return pl.BlockSpec(memory_space=pltpu.VMEM)


def hbm():
    return pl.BlockSpec(memory_space=pltpu.HBM)


def folded_hot(cells, depth, lines, fold):
    few = lines // fold
    line = jnp.right_shift(cells, depth.bit_length() - 1)
    own = jnp.bitwise_and(line, few - 1)
    key = jnp.right_shift(line, few.bit_length() - 1) * depth + jnp.bitwise_and(cells, depth - 1)
    at = lax.broadcasted_iota(jnp.int32, (fold * depth, cells.shape[1]), 0)
    return jnp.where(at == key, 1.0, 0.0).astype(jnp.bfloat16), own


def root_first(count):
    root = count * 9 // 16
    return [root] + [index for index in range(count) if index != root]


def trace_kernel(dims, row_swaps, target_hbm, cell_hbm, field_hbm, tile_hbm, *rest):
    comps, width_x, width_y, depth, rows, cols = dims
    row_faces, col_faces = rest[:row_swaps], rest[row_swaps : row_swaps + 2]
    target_ref, cell_ref, field_ref, lhs_ref, tile_ref, side_ref, arrived, left_sem = rest[
        row_swaps + 2 :
    ]
    lines = width_x * width_y
    nodes = cell_ref.shape[1]
    slot_len = nodes // cols
    chunks, few = lhs_ref.shape[:2]
    fold = lines // few
    span = comps // chunks
    copies = [pltpu.make_async_copy(cell_hbm, cell_ref, arrived.at[chunks])]
    for chunk in range(chunks):
        part = pl.ds(chunk * span, span)
        copies.append(
            pltpu.make_async_copy(field_hbm.at[part], field_ref.at[part], arrived.at[chunk])
        )
    copies.append(pltpu.make_async_copy(target_hbm, target_ref, arrived.at[chunks + 1]))
    for copy in copies:
        copy.start()
    sent = []
    copies[0].wait()
    hot, own = folded_hot(cell_ref[...], depth, lines, fold)
    own = jnp.broadcast_to(own, (8, nodes))
    flat = field_ref.reshape(comps * lines, depth)
    found = []
    for chunk in range(chunks):
        copies[1 + chunk].wait()
        for line in range(lines):
            lhs_ref[chunk, line % few, :, pl.ds(line // few * depth, depth)] = flat[
                pl.ds(chunk * span * lines + line, span, stride=lines), :
            ].astype(jnp.bfloat16)
        total = jnp.zeros((span // 8, 8, nodes), jnp.float32)
        group = min(4, few)
        for first in range(0, few, group):
            block = jnp.dot(
                lhs_ref[chunk, first : first + group].reshape(group * span, fold * depth),
                hot,
                preferred_element_type=jnp.float32,
            ).reshape(group, span // 8, 8, nodes)
            for line in range(group):
                total = jnp.where((own == first + line)[None], block[line], total)
        found.append(total.reshape(span, nodes))
    col_odd = lax.rem(lax.axis_index("col"), 2)
    for swap, face_ref in enumerate(col_faces):
        layer = jnp.where(col_odd == swap, width_x - 1, 0)
        start = pl.multiple_of(layer * width_y, width_y)
        sent.append(
            pltpu.make_async_copy(
                field_ref.at[:, pl.ds(start, width_y), :], face_ref, left_sem.at[swap]
            )
        )
        sent[-1].start()
    row_odd = lax.rem(lax.axis_index("row"), 2)
    for swap, face_ref in enumerate(row_faces):
        low, high = (
            flat[pl.ds(layer, comps * width_x, stride=width_y), :] for layer in (0, width_y - 1)
        )
        side_ref[swap] = jnp.where(row_odd == swap, high, low).astype(jnp.bfloat16)
        sent.append(pltpu.make_async_copy(side_ref.at[swap], face_ref, left_sem.at[2 + swap]))
        sent[-1].start()
    by_node = jnp.concatenate(found, axis=0).T
    copies[-1].wait()
    left_len = min(slot_len, TILE_ROWS)
    for slot in range(cols):
        piece = by_node[slot * slot_len : (slot + 1) * slot_len]
        left = piece[:left_len]
        right = piece[left_len:]
        if left_len < TILE_ROWS:
            left = jnp.concatenate(
                [left, jnp.zeros((TILE_ROWS - left_len, comps), jnp.float32)], axis=0
            )
        gap = TILE_ROWS - (slot_len - left_len)
        if slot_len == left_len:
            right = jnp.zeros((TILE_ROWS, comps), jnp.float32)
        elif gap:
            right = jnp.concatenate([right, jnp.zeros((gap, comps), jnp.float32)], axis=0)
        tile = jnp.concatenate([left, right], axis=1).astype(jnp.bfloat16)
        for row in range(rows):
            tile_ref[row * cols + target_ref[0, slot]] = tile
    sent.append(pltpu.make_async_copy(tile_ref, tile_hbm, left_sem.at[2 + row_swaps]))
    sent[-1].start()
    for copy in sent:
        copy.wait()


def corner_kernel(dims, first_ref, second_ref, *out_refs):
    comps, width_x, width_y = dims[:3]
    odd = lax.rem(lax.axis_index("row"), 2)
    for swap, out_ref in enumerate(out_refs):
        for index, ref in enumerate((first_ref, second_ref)):
            low, high = (ref[pl.ds(layer, comps, stride=width_y), :] for layer in (0, width_y - 1))
            out_ref[pl.ds(index * comps, comps), :] = jnp.where(odd == swap, high, low).astype(
                out_ref.dtype
            )


def unpack_tiles(tiles, slot_len, comps):
    left_len = min(slot_len, TILE_ROWS)
    parts = [tiles[:, :left_len, :comps]]
    if slot_len > left_len:
        parts.append(tiles[:, : slot_len - left_len, comps:])
    both = jnp.concatenate(parts, axis=1) if len(parts) > 1 else parts[0]
    return both.reshape(tiles.shape[0] * slot_len, comps)


def boundary_kernel(slot_len, own_rows, trace_ref, real_ref, imag_ref, row_ref, out_ref):
    if len(trace_ref.shape) == 3:
        traces = unpack_tiles(
            trace_ref[...].astype(jnp.float32), slot_len, trace_ref.shape[2] // 2
        )
    else:
        traces = trace_ref[...].astype(jnp.float32)
    comps = traces.shape[1]
    angles = comps // 2
    turned = jnp.concatenate([-traces[:, angles:], traces[:, :angles]], axis=1)
    image = jnp.dot(
        real_ref[...], traces.astype(jnp.bfloat16), preferred_element_type=jnp.float32
    ) + jnp.dot(imag_ref[...], turned.astype(jnp.bfloat16), preferred_element_type=jnp.float32)
    image = image.reshape(image.shape[0] // own_rows, own_rows, comps)
    half = own_rows // 2
    packed = jnp.concatenate([image[:, :half], image[:, half:]], axis=2).astype(out_ref.dtype)
    for place, col in enumerate(root_first(packed.shape[0])):
        out_ref[place] = packed[col]


def shifted_z(values, step):
    rows, depth = values.shape
    at_z = lax.broadcasted_iota(jnp.int32, (rows, depth), 1)
    outside = at_z == (0 if step == 1 else depth - 1)
    return jnp.where(outside, 0.0, pltpu.roll(values, step % depth, 1))


def side_z(values):
    return shifted_z(values, 1) + shifted_z(values, -1)


def volume_kernel(dims, row_swaps, *refs):
    comps, width_x, width_y, depth, rows, cols = dims
    field_ref, medium_ref, flux_ref, cell_ref = refs[:4]
    row_refs = refs[4 : 4 + row_swaps]
    first_ref, second_ref = refs[4 + row_swaps : 6 + row_swaps]
    out_hbm, edge_ref, lhs_ref, taken_ref, out_ref, side_ref, sent = refs[6 + row_swaps :]
    for index, row_ref in enumerate(row_refs):
        side_ref[index] = row_ref[...].astype(jnp.float32)
    lines = width_x * width_y
    nodes = cell_ref.shape[1]
    fold = 2
    few = lines // fold
    hot, own = folded_hot(cell_ref[...], depth, lines, fold)
    at_line = lax.broadcasted_iota(jnp.int32, (few, nodes), 0)
    line_hot = jnp.where(at_line == own, 1.0, 0.0)
    for comp in range(comps):
        lhs_ref[pl.ds(comp * few, few), :] = (
            line_hot * jnp.broadcast_to(flux_ref[comp], (few, nodes))
        ).astype(jnp.bfloat16)
    taken_ref[...] = lax.dot_general(
        lhs_ref[...], hot, (((1,), (1,)), ((), ())), preferred_element_type=jnp.float32
    )

    row_odd = lax.rem(lax.axis_index("row"), 2) == 1
    col_odd = lax.rem(lax.axis_index("col"), 2) == 1
    shape = (width_y, depth)
    at_y = lax.broadcasted_iota(jnp.int32, shape, 0)
    low_y, high_y = at_y == 0, at_y == width_y - 1
    weight = [1.0 / 12.0 + medium_ref[pl.ds(x * width_y, width_y), :] / 27.0 for x in range(width_x)]
    from_first = jnp.logical_or(
        jnp.logical_and(high_y, jnp.logical_not(row_odd)), jnp.logical_and(low_y, row_odd)
    )

    def side_y(values, ends):
        lower = jnp.where(low_y, ends, pltpu.roll(values, 1, 0))
        upper = jnp.where(high_y, ends, pltpu.roll(values, width_y - 1, 0))
        return lower + upper

    def wide(ref, index):
        return jnp.broadcast_to(ref[pl.ds(index, 1), :], shape)

    def component(comp):
        base = comp * lines
        planes = [
            field_ref[pl.ds(base + x * width_y, width_y), :]
            for x in range(width_x)
        ]
        face = pl.ds(comp * width_y, width_y)
        first, second = first_ref[face, :], second_ref[face, :]
        planes = (
            [jnp.where(col_odd, first, second)] + planes + [jnp.where(col_odd, second, first)]
        )
        ends = []
        for x in range(width_x):
            line = [wide(side_ref.at[index], comp * width_x + x) for index in range(row_swaps)]
            ends.append(jnp.where(from_first, line[0], line[1] if row_swaps > 1 else 0.0))
        none = jnp.zeros(shape, jnp.float32)
        ends = [none] + ends + [none]
        for x in range(width_x):
            centre = planes[x + 1]
            sides = planes[x] + planes[x + 2]
            over_x = 2.0 * centre + sides
            ends_x = 2.0 * ends[x + 1] + (ends[x] + ends[x + 2])
            over_xy = 2.0 * over_x + side_y(over_x, ends_x)
            over_xyz = 2.0 * over_xy + side_z(over_xy)
            near = sides + side_y(centre, ends[x + 1]) + side_z(centre)
            here = pl.ds(base + x * width_y, width_y)
            image = (
                (10.0 / 3.0) * centre
                + (1.0 / 3.0) * near
                - weight[x] * over_xyz
                - taken_ref[
                    pl.ds(
                        pl.multiple_of(comp * few + x * width_y % few, width_y), width_y
                    ),
                    pl.ds(x * width_y // few * depth, depth),
                ]
            )
            out_ref[here, :] = image
            for side in range(2):
                if x == side * (width_x - 1):
                    edge_ref[side, face, :] = image

    steps = sent.shape[0]
    together = comps // steps
    copies = []
    for step in range(steps):
        for comp in range(step * together, (step + 1) * together):
            component(comp)
        here = pl.ds(step * together * lines, together * lines)
        copies.append(
            pltpu.make_async_copy(out_ref.at[here, :], out_hbm.at[here, :], sent.at[step])
        )
        copies[-1].start()
    for copy in copies:
        copy.wait()


def last_kernel(
    dims, row_swaps, part_ref, medium_ref, edge_ref, *refs
):
    comps, width_x, width_y, depth, rows, cols = dims
    corner_refs = refs[:row_swaps]
    image_ref, volume_ref, plane_ref, total_ref, sent = refs[row_swaps + 1 :]
    row_odd = lax.rem(lax.axis_index("row"), 2)
    col_odd = lax.rem(lax.axis_index("col"), 2) == 1
    copies = []
    at_row = lax.broadcasted_iota(jnp.int32, (width_y, depth), 0)
    for side in range(2):
        at_x = side * (width_x - 1)
        weight = 1.0 / 12.0 + medium_ref[pl.ds(at_x * width_y, width_y), :] / 27.0
        plane = edge_ref[side].reshape(comps, width_y, depth)
        for index in range(row_swaps):
            first = corner_refs[index][pl.ds(0, comps), :].astype(jnp.float32)
            second = corner_refs[index][pl.ds(comps, comps), :].astype(jnp.float32)
            line = jnp.where(col_odd, second, first) if side else jnp.where(col_odd, first, second)
            line = 2.0 * line + side_z(line)
            at_y = jnp.where(row_odd == index, width_y - 1, 0)
            share = jnp.where(at_row == at_y, weight, 0.0)
            plane = plane - share[None] * line[:, None, :]
        plane_ref[side] = plane.reshape(comps * width_y, depth)
        copies.append(
            pltpu.make_async_copy(
                plane_ref.at[side].reshape(comps, width_y, depth),
                volume_ref.at[:, pl.ds(at_x * width_y, width_y), :],
                sent.at[side],
            )
        )
        copies[-1].start()
    total = jnp.sum(part_ref[...].astype(jnp.float32), axis=0)
    half, lanes = total.shape
    total_ref[:half] = total[:, : lanes // 2]
    total_ref[half:] = total[:, lanes // 2 :]
    copies.append(pltpu.make_async_copy(total_ref, image_ref, sent.at[2]))
    copies[-1].start()
    for copy in copies:
        copy.wait()


def swap_pairs(count, swap):
    pairs = []
    for low in range(swap, count - 1, 2):
        pairs += [(low, low + 1), (low + 1, low)]
    return pairs


def on_device(wave_field, medium_term, node_flux, node_cell, block_target, boundary_matrix):
    comps, width_x, width_y, depth = wave_field.shape
    rows, cols = lax.axis_size("row"), lax.axis_size("col")
    dims = (comps, width_x, width_y, depth, rows, cols)
    lines = width_x * width_y
    nodes = node_cell.shape[-1]
    slot_len = nodes // cols
    row_swaps = 1 if rows == 2 else 2
    slab_rows, span = boundary_matrix.shape[1:]
    own_rows = slab_rows // cols
    f32, bf16 = jnp.float32, jnp.bfloat16
    params = pltpu.CompilerParams(vmem_limit_bytes=SMALL)

    chunks, fold = 2, 4
    field = wave_field.reshape(comps * lines, depth)
    cells = node_cell.reshape(1, nodes)
    targets = block_target.reshape(1, cols)
    flux = node_flux.reshape(comps, 1, nodes)
    medium = medium_term.reshape(lines, depth)

    tiles, *faces = pl.pallas_call(
        functools.partial(trace_kernel, dims, row_swaps),
        out_shape=[jax.ShapeDtypeStruct((rows * cols, TILE_ROWS, 2 * comps), bf16)]
        + [jax.ShapeDtypeStruct((comps * width_x, depth), bf16)] * row_swaps
        + [jax.ShapeDtypeStruct((comps, width_y, depth), f32)] * 2,
        in_specs=[hbm()] * 3,
        out_specs=[hbm()] * (3 + row_swaps),
        scratch_shapes=[
            pltpu.SMEM((1, cols), jnp.int32),
            pltpu.VMEM((1, nodes), jnp.int32),
            pltpu.VMEM((comps, lines, depth), f32),
            pltpu.VMEM((chunks, lines // fold, comps // chunks, fold * depth), bf16),
            pltpu.VMEM((rows * cols, TILE_ROWS, 2 * comps), bf16),
            pltpu.VMEM((row_swaps, comps * width_x, depth), bf16),
            pltpu.SemaphoreType.DMA((chunks + 2,)),
            pltpu.SemaphoreType.DMA((3 + row_swaps,)),
        ],
        compiler_params=pltpu.CompilerParams(vmem_limit_bytes=WHOLE),
        name="traces",
    )(targets, cells, field.reshape(comps, lines, depth))
    col_sides = [
        lax.ppermute(face, "col", swap_pairs(cols, swap)).reshape(comps * width_y, depth)
        for swap, face in enumerate(faces[row_swaps : row_swaps + 2])
    ]
    row_sides = [
        lax.ppermute(face, "row", swap_pairs(rows, swap))
        for swap, face in enumerate(faces[:row_swaps])
    ]
    received = lax.all_to_all(tiles, ("row", "col"), 0, 0, tiled=True)

    if slot_len % 8:
        received = unpack_tiles(received, slot_len, comps)
    shares = pl.pallas_call(
        functools.partial(boundary_kernel, slot_len, own_rows),
        out_shape=jax.ShapeDtypeStruct((cols, own_rows // 2, 2 * comps), bf16),
        in_specs=[vmem()] * 4,
        out_specs=vmem(),
        compiler_params=params,
        name="boundary",
    )(received, boundary_matrix[0], boundary_matrix[1], row_sides[0])
    shares = lax.all_to_all(
        shares, "col", 0, 0, tiled=True, axis_index_groups=[root_first(cols)]
    )

    corners = pl.pallas_call(
        functools.partial(corner_kernel, dims),
        out_shape=[jax.ShapeDtypeStruct((2 * comps, depth), bf16)] * row_swaps,
        in_specs=[vmem()] * 2,
        out_specs=[vmem()] * row_swaps,
        compiler_params=params,
        name="corners",
    )(*col_sides)
    corner_sides = [
        lax.ppermute(lines_of, "row", swap_pairs(rows, swap))
        for swap, lines_of in enumerate(corners)
    ]

    volume, edges = pl.pallas_call(
        functools.partial(volume_kernel, dims, row_swaps),
        out_shape=[
            jax.ShapeDtypeStruct((comps * lines, depth), f32),
            jax.ShapeDtypeStruct((2, comps * width_y, depth), f32),
        ],
        in_specs=[vmem()] * (6 + row_swaps),
        out_specs=[hbm(), vmem()],
        scratch_shapes=[
            pltpu.VMEM((comps * lines // 2, nodes), bf16),
            pltpu.VMEM((comps * lines // 2, 2 * depth), f32),
            pltpu.VMEM((comps * lines, depth), f32),
            pltpu.VMEM((row_swaps, comps * width_x, depth), f32),
            pltpu.SemaphoreType.DMA((8,)),
        ],
        compiler_params=params,
        name="volume",
    )(field, medium, flux, cells, *row_sides, *col_sides)

    boundary_image, volume = pl.pallas_call(
        functools.partial(last_kernel, dims, row_swaps),
        out_shape=[
            jax.ShapeDtypeStruct((own_rows, comps), f32),
            jax.ShapeDtypeStruct((comps, lines, depth), f32),
        ],
        in_specs=[vmem()] * (3 + row_swaps) + [hbm()],
        out_specs=[hbm(), hbm()],
        scratch_shapes=[
            pltpu.VMEM((2, comps * width_y, depth), f32),
            pltpu.VMEM((own_rows, comps), f32),
            pltpu.SemaphoreType.DMA((3,)),
        ],
        input_output_aliases={3 + row_swaps: 1},
        compiler_params=params,
        name="last",
    )(shares, medium, edges, *corner_sides, volume.reshape(comps, lines, depth))
    return (volume.reshape(comps, width_x, width_y, depth), boundary_image)


def solution(mesh):
    in_specs = (
        P(None, "col", "row", None),
        P("col", "row", None),
        P(None, "col", "row", None),
        P("col", "row", None),
        P("col", "row", None),
        P(None, "row", "col"),
    )
    out_specs = (P(None, "col", "row", None), P(("row", "col"), None))
    return jax.shard_map(
        on_device, mesh=mesh, in_specs=in_specs, out_specs=out_specs, check_vma=False
    )
```

```python
import functools

import jax
import jax.numpy as jnp
from jax import lax
from jax.experimental import pallas as pl
from jax.experimental.pallas import tpu as pltpu
from jax.sharding import PartitionSpec as P

TILE_ROWS = 16
SMALL = 8 * 2**20
WHOLE = 64560 * 2**10


def vmem():
    return pl.BlockSpec(memory_space=pltpu.VMEM)


def hbm():
    return pl.BlockSpec(memory_space=pltpu.HBM)


def folded_hot(cells, depth, lines, fold):
    few = lines // fold
    line = jnp.right_shift(cells, depth.bit_length() - 1)
    own = jnp.bitwise_and(line, few - 1)
    key = jnp.right_shift(line, few.bit_length() - 1) * depth + jnp.bitwise_and(cells, depth - 1)
    at = lax.broadcasted_iota(jnp.int32, (fold * depth, cells.shape[1]), 0)
    return jnp.where(at == key, 1.0, 0.0).astype(jnp.bfloat16), own


def root_first(count):
    root = count * 9 // 16
    return [root] + [index for index in range(count) if index != root]


def trace_kernel(dims, row_swaps, target_hbm, cell_hbm, field_hbm, tile_hbm, *rest):
    comps, width_x, width_y, depth, rows, cols = dims
    row_faces, col_faces = rest[:row_swaps], rest[row_swaps : row_swaps + 2]
    target_ref, cell_ref, field_ref, lhs_ref, tile_ref, side_ref, arrived, left_sem = rest[
        row_swaps + 2 :
    ]
    lines = width_x * width_y
    nodes = cell_ref.shape[1]
    slot_len = nodes // cols
    chunks, few = lhs_ref.shape[:2]
    fold = lines // few
    span = comps // chunks
    copies = [pltpu.make_async_copy(cell_hbm, cell_ref, arrived.at[chunks])]
    for chunk in range(chunks):
        part = pl.ds(chunk * span, span)
        copies.append(
            pltpu.make_async_copy(field_hbm.at[part], field_ref.at[part], arrived.at[chunk])
        )
    copies.append(pltpu.make_async_copy(target_hbm, target_ref, arrived.at[chunks + 1]))
    for copy in copies:
        copy.start()
    sent = []
    copies[0].wait()
    hot, own = folded_hot(cell_ref[...], depth, lines, fold)
    own = jnp.broadcast_to(own, (8, nodes))
    flat = field_ref.reshape(comps * lines, depth)
    found = []
    for chunk in range(chunks):
        copies[1 + chunk].wait()
        for line in range(lines):
            lhs_ref[chunk, line % few, :, pl.ds(line // few * depth, depth)] = flat[
                pl.ds(chunk * span * lines + line, span, stride=lines), :
            ].astype(jnp.bfloat16)
        total = jnp.zeros((span // 8, 8, nodes), jnp.float32)
        group = min(4, few)
        for first in range(0, few, group):
            block = jnp.dot(
                lhs_ref[chunk, first : first + group].reshape(group * span, fold * depth),
                hot,
                preferred_element_type=jnp.float32,
            ).reshape(group, span // 8, 8, nodes)
            for line in range(group):
                total = jnp.where((own == first + line)[None], block[line], total)
        found.append(total.reshape(span, nodes))
    col_odd = lax.rem(lax.axis_index("col"), 2)
    for swap, face_ref in enumerate(col_faces):
        layer = jnp.where(col_odd == swap, width_x - 1, 0)
        start = pl.multiple_of(layer * width_y, width_y)
        sent.append(
            pltpu.make_async_copy(
                field_ref.at[:, pl.ds(start, width_y), :], face_ref, left_sem.at[swap]
            )
        )
        sent[-1].start()
    by_node = jnp.concatenate(found, axis=0).T
    copies[-1].wait()
    left_len = min(slot_len, TILE_ROWS)
    for slot in range(cols):
        piece = by_node[slot * slot_len : (slot + 1) * slot_len]
        left = piece[:left_len]
        right = piece[left_len:]
        if left_len < TILE_ROWS:
            left = jnp.concatenate(
                [left, jnp.zeros((TILE_ROWS - left_len, comps), jnp.float32)], axis=0
            )
        gap = TILE_ROWS - (slot_len - left_len)
        if slot_len == left_len:
            right = jnp.zeros((TILE_ROWS, comps), jnp.float32)
        elif gap:
            right = jnp.concatenate([right, jnp.zeros((gap, comps), jnp.float32)], axis=0)
        tile = jnp.concatenate([left, right], axis=1).astype(jnp.bfloat16)
        for row in range(rows):
            tile_ref[row * cols + target_ref[0, slot]] = tile
    sent.append(pltpu.make_async_copy(tile_ref, tile_hbm, left_sem.at[2 + row_swaps]))
    sent[-1].start()
    row_odd = lax.rem(lax.axis_index("row"), 2)
    for swap, face_ref in enumerate(row_faces):
        low, high = (
            flat[pl.ds(layer, comps * width_x, stride=width_y), :] for layer in (0, width_y - 1)
        )
        side_ref[swap] = jnp.where(row_odd == swap, high, low).astype(jnp.bfloat16)
        sent.append(pltpu.make_async_copy(side_ref.at[swap], face_ref, left_sem.at[2 + swap]))
        sent[-1].start()
    for copy in sent:
        copy.wait()


def corner_kernel(dims, first_ref, second_ref, *out_refs):
    comps, width_x, width_y = dims[:3]
    odd = lax.rem(lax.axis_index("row"), 2)
    for swap, out_ref in enumerate(out_refs):
        for index, ref in enumerate((first_ref, second_ref)):
            low, high = (ref[pl.ds(layer, comps, stride=width_y), :] for layer in (0, width_y - 1))
            line = jnp.where(odd == swap, high, low)
            out_ref[pl.ds(index * comps, comps), :] = (2.0 * line + side_z(line)).astype(
                out_ref.dtype
            )


def unpack_tiles(tiles, slot_len, comps):
    left_len = min(slot_len, TILE_ROWS)
    parts = [tiles[:, :left_len, :comps]]
    if slot_len > left_len:
        parts.append(tiles[:, : slot_len - left_len, comps:])
    both = jnp.concatenate(parts, axis=1) if len(parts) > 1 else parts[0]
    return both.reshape(tiles.shape[0] * slot_len, comps)


def boundary_kernel(slot_len, own_rows, trace_ref, real_ref, imag_ref, row_ref, out_ref):
    if len(trace_ref.shape) == 3:
        traces = unpack_tiles(
            trace_ref[...].astype(jnp.float32), slot_len, trace_ref.shape[2] // 2
        )
    else:
        traces = trace_ref[...].astype(jnp.float32)
    comps = traces.shape[1]
    angles = comps // 2
    traces = traces.astype(jnp.bfloat16)
    image = jnp.dot(real_ref[...], traces, preferred_element_type=jnp.float32)
    other = jnp.dot(imag_ref[...], traces, preferred_element_type=jnp.float32)
    image = image + jnp.concatenate([-other[:, angles:], other[:, :angles]], axis=1)
    image = image.reshape(image.shape[0] // own_rows, own_rows, comps)
    half = own_rows // 2
    packed = jnp.concatenate([image[:, :half], image[:, half:]], axis=2).astype(out_ref.dtype)
    for place, col in enumerate(root_first(packed.shape[0])):
        out_ref[place] = packed[col]


def shifted_z(values, step):
    rows, depth = values.shape
    at_z = lax.broadcasted_iota(jnp.int32, (rows, depth), 1)
    outside = at_z == (0 if step == 1 else depth - 1)
    return jnp.where(outside, 0.0, pltpu.roll(values, step % depth, 1))


def side_z(values):
    return shifted_z(values, 1) + shifted_z(values, -1)


def volume_kernel(dims, row_swaps, *refs):
    comps, width_x, width_y, depth, rows, cols = dims
    field_ref, medium_ref, flux_ref, cell_ref = refs[:4]
    row_refs = refs[4 : 4 + row_swaps]
    first_ref, second_ref = refs[4 + row_swaps : 6 + row_swaps]
    out_hbm, edge_ref, lhs_ref, taken_ref, out_ref, side_ref, sent = refs[6 + row_swaps :]
    for index, row_ref in enumerate(row_refs):
        side_ref[index] = row_ref[...].astype(jnp.float32)
    lines = width_x * width_y
    nodes = cell_ref.shape[1]
    fold = 2
    few = lines // fold
    hot, own = folded_hot(cell_ref[...], depth, lines, fold)
    at_line = lax.broadcasted_iota(jnp.int32, (few, nodes), 0)
    line_hot = jnp.where(at_line == own, 1.0, 0.0)
    for comp in range(comps):
        lhs_ref[pl.ds(comp * few, few), :] = (
            line_hot * jnp.broadcast_to(flux_ref[comp], (few, nodes))
        ).astype(jnp.bfloat16)
    taken_ref[...] = lax.dot_general(
        lhs_ref[...], hot, (((1,), (1,)), ((), ())), preferred_element_type=jnp.float32
    )

    row_odd = lax.rem(lax.axis_index("row"), 2) == 1
    col_odd = lax.rem(lax.axis_index("col"), 2) == 1
    shape = (width_y, depth)
    at_y = lax.broadcasted_iota(jnp.int32, shape, 0)
    low_y, high_y = at_y == 0, at_y == width_y - 1
    weight = [1.0 / 12.0 + medium_ref[pl.ds(x * width_y, width_y), :] / 27.0 for x in range(width_x)]
    from_first = jnp.logical_or(
        jnp.logical_and(high_y, jnp.logical_not(row_odd)), jnp.logical_and(low_y, row_odd)
    )

    def side_y(values, ends):
        lower = jnp.where(low_y, ends, pltpu.roll(values, 1, 0))
        upper = jnp.where(high_y, ends, pltpu.roll(values, width_y - 1, 0))
        return lower + upper

    def wide(ref, index):
        return jnp.broadcast_to(ref[pl.ds(index, 1), :], shape)

    def component(comp):
        base = comp * lines
        planes = [
            field_ref[pl.ds(base + x * width_y, width_y), :]
            for x in range(width_x)
        ]
        face = pl.ds(comp * width_y, width_y)
        first, second = first_ref[face, :], second_ref[face, :]
        planes = (
            [jnp.where(col_odd, first, second)] + planes + [jnp.where(col_odd, second, first)]
        )
        ends = []
        for x in range(width_x):
            line = [wide(side_ref.at[index], comp * width_x + x) for index in range(row_swaps)]
            ends.append(jnp.where(from_first, line[0], line[1] if row_swaps > 1 else 0.0))
        none = jnp.zeros(shape, jnp.float32)
        ends = [none] + ends + [none]
        for x in range(width_x):
            centre = planes[x + 1]
            sides = planes[x] + planes[x + 2]
            over_x = 2.0 * centre + sides
            ends_x = 2.0 * ends[x + 1] + (ends[x] + ends[x + 2])
            over_xy = 2.0 * over_x + side_y(over_x, ends_x)
            over_xyz = 2.0 * over_xy + side_z(over_xy)
            near = sides + side_y(centre, ends[x + 1]) + side_z(centre)
            here = pl.ds(base + x * width_y, width_y)
            image = (
                (10.0 / 3.0) * centre
                + (1.0 / 3.0) * near
                - weight[x] * over_xyz
                - taken_ref[
                    pl.ds(
                        pl.multiple_of(comp * few + x * width_y % few, width_y), width_y
                    ),
                    pl.ds(x * width_y // few * depth, depth),
                ]
            )
            out_ref[here, :] = image
            for side in range(2):
                if x == side * (width_x - 1):
                    edge_ref[side, face, :] = image

    steps = sent.shape[0]
    together = comps // steps
    copies = []
    for step in range(steps):
        for comp in range(step * together, (step + 1) * together):
            component(comp)
        here = pl.ds(step * together * lines, together * lines)
        copies.append(
            pltpu.make_async_copy(out_ref.at[here, :], out_hbm.at[here, :], sent.at[step])
        )
        copies[-1].start()
    for copy in copies:
        copy.wait()


def last_kernel(
    dims, row_swaps, part_ref, medium_ref, edge_ref, *refs
):
    comps, width_x, width_y, depth, rows, cols = dims
    corner_refs = refs[:row_swaps]
    image_ref, volume_ref, plane_ref, total_ref, sent = refs[row_swaps + 1 :]
    row_odd = lax.rem(lax.axis_index("row"), 2)
    col_odd = lax.rem(lax.axis_index("col"), 2) == 1
    copies = []
    at_row = lax.broadcasted_iota(jnp.int32, (width_y, depth), 0)
    for side in range(2):
        at_x = side * (width_x - 1)
        weight = 1.0 / 12.0 + medium_ref[pl.ds(at_x * width_y, width_y), :] / 27.0
        plane = edge_ref[side].reshape(comps, width_y, depth)
        for index in range(row_swaps):
            first = corner_refs[index][pl.ds(0, comps), :].astype(jnp.float32)
            second = corner_refs[index][pl.ds(comps, comps), :].astype(jnp.float32)
            line = jnp.where(col_odd, second, first) if side else jnp.where(col_odd, first, second)
            at_y = jnp.where(row_odd == index, width_y - 1, 0)
            share = jnp.where(at_row == at_y, weight, 0.0)
            plane = plane - share[None] * line[:, None, :]
        plane_ref[side] = plane.reshape(comps * width_y, depth)
        copies.append(
            pltpu.make_async_copy(
                plane_ref.at[side].reshape(comps, width_y, depth),
                volume_ref.at[:, pl.ds(at_x * width_y, width_y), :],
                sent.at[side],
            )
        )
        copies[-1].start()
    total = jnp.sum(part_ref[...].astype(jnp.float32), axis=0)
    half, lanes = total.shape
    total_ref[:half] = total[:, : lanes // 2]
    total_ref[half:] = total[:, lanes // 2 :]
    copies.append(pltpu.make_async_copy(total_ref, image_ref, sent.at[2]))
    copies[-1].start()
    for copy in copies:
        copy.wait()


def swap_pairs(count, swap):
    pairs = []
    for low in range(swap, count - 1, 2):
        pairs += [(low, low + 1), (low + 1, low)]
    return pairs


def on_device(wave_field, medium_term, node_flux, node_cell, block_target, boundary_matrix):
    comps, width_x, width_y, depth = wave_field.shape
    rows, cols = lax.axis_size("row"), lax.axis_size("col")
    dims = (comps, width_x, width_y, depth, rows, cols)
    lines = width_x * width_y
    nodes = node_cell.shape[-1]
    slot_len = nodes // cols
    row_swaps = 1 if rows == 2 else 2
    slab_rows, span = boundary_matrix.shape[1:]
    own_rows = slab_rows // cols
    f32, bf16 = jnp.float32, jnp.bfloat16
    params = pltpu.CompilerParams(vmem_limit_bytes=SMALL)

    chunks, fold = 2, 4
    field = wave_field.reshape(comps * lines, depth)
    cells = node_cell.reshape(1, nodes)
    targets = block_target.reshape(1, cols)
    flux = node_flux.reshape(comps, 1, nodes)
    medium = medium_term.reshape(lines, depth)

    tiles, *faces = pl.pallas_call(
        functools.partial(trace_kernel, dims, row_swaps),
        out_shape=[jax.ShapeDtypeStruct((rows * cols, TILE_ROWS, 2 * comps), bf16)]
        + [jax.ShapeDtypeStruct((comps * width_x, depth), bf16)] * row_swaps
        + [jax.ShapeDtypeStruct((comps, width_y, depth), f32)] * 2,
        in_specs=[hbm()] * 3,
        out_specs=[hbm()] * (3 + row_swaps),
        scratch_shapes=[
            pltpu.SMEM((1, cols), jnp.int32),
            pltpu.VMEM((1, nodes), jnp.int32),
            pltpu.VMEM((comps, lines, depth), f32),
            pltpu.VMEM((chunks, lines // fold, comps // chunks, fold * depth), bf16),
            pltpu.VMEM((rows * cols, TILE_ROWS, 2 * comps), bf16),
            pltpu.VMEM((row_swaps, comps * width_x, depth), bf16),
            pltpu.SemaphoreType.DMA((chunks + 2,)),
            pltpu.SemaphoreType.DMA((3 + row_swaps,)),
        ],
        compiler_params=pltpu.CompilerParams(vmem_limit_bytes=WHOLE),
        name="traces",
    )(targets, cells, field.reshape(comps, lines, depth))
    col_sides = [
        lax.ppermute(face, "col", swap_pairs(cols, swap)).reshape(comps * width_y, depth)
        for swap, face in enumerate(faces[row_swaps : row_swaps + 2])
    ]
    row_sides = [
        lax.ppermute(face, "row", swap_pairs(rows, swap))
        for swap, face in enumerate(faces[:row_swaps])
    ]
    received = lax.all_to_all(tiles, ("row", "col"), 0, 0, tiled=True)

    if slot_len % 8:
        received = unpack_tiles(received, slot_len, comps)
    shares = pl.pallas_call(
        functools.partial(boundary_kernel, slot_len, own_rows),
        out_shape=jax.ShapeDtypeStruct((cols, own_rows // 2, 2 * comps), bf16),
        in_specs=[vmem()] * 4,
        out_specs=vmem(),
        compiler_params=params,
        name="boundary",
    )(received, boundary_matrix[0], boundary_matrix[1], row_sides[0])
    shares = lax.all_to_all(
        shares, "col", 0, 0, tiled=True, axis_index_groups=[root_first(cols)]
    )

    corners = pl.pallas_call(
        functools.partial(corner_kernel, dims),
        out_shape=[jax.ShapeDtypeStruct((2 * comps, depth), bf16)] * row_swaps,
        in_specs=[vmem()] * 2,
        out_specs=[vmem()] * row_swaps,
        compiler_params=params,
        name="corners",
    )(*col_sides)
    corner_sides = [
        lax.ppermute(lines_of, "row", swap_pairs(rows, swap))
        for swap, lines_of in enumerate(corners)
    ]

    volume, edges = pl.pallas_call(
        functools.partial(volume_kernel, dims, row_swaps),
        out_shape=[
            jax.ShapeDtypeStruct((comps * lines, depth), f32),
            jax.ShapeDtypeStruct((2, comps * width_y, depth), f32),
        ],
        in_specs=[vmem()] * (6 + row_swaps),
        out_specs=[hbm(), vmem()],
        scratch_shapes=[
            pltpu.VMEM((comps * lines // 2, nodes), bf16),
            pltpu.VMEM((comps * lines // 2, 2 * depth), f32),
            pltpu.VMEM((comps * lines, depth), f32),
            pltpu.VMEM((row_swaps, comps * width_x, depth), f32),
            pltpu.SemaphoreType.DMA((8,)),
        ],
        compiler_params=params,
        name="volume",
    )(field, medium, flux, cells, *row_sides, *col_sides)

    boundary_image, volume = pl.pallas_call(
        functools.partial(last_kernel, dims, row_swaps),
        out_shape=[
            jax.ShapeDtypeStruct((own_rows, comps), f32),
            jax.ShapeDtypeStruct((comps, lines, depth), f32),
        ],
        in_specs=[vmem()] * (3 + row_swaps) + [hbm()],
        out_specs=[hbm(), hbm()],
        scratch_shapes=[
            pltpu.VMEM((2, comps * width_y, depth), f32),
            pltpu.VMEM((own_rows, comps), f32),
            pltpu.SemaphoreType.DMA((3,)),
        ],
        input_output_aliases={3 + row_swaps: 1},
        compiler_params=params,
        name="last",
    )(shares, medium, edges, *corner_sides, volume.reshape(comps, lines, depth))
    return (volume.reshape(comps, width_x, width_y, depth), boundary_image)


def solution(mesh):
    in_specs = (
        P(None, "col", "row", None),
        P("col", "row", None),
        P(None, "col", "row", None),
        P("col", "row", None),
        P("col", "row", None),
        P(None, "row", "col"),
    )
    out_specs = (P(None, "col", "row", None), P(("row", "col"), None))
    return jax.shard_map(
        on_device, mesh=mesh, in_specs=in_specs, out_specs=out_specs, check_vma=False
    )
```

```python
import functools

import jax
import jax.numpy as jnp
from jax import lax
from jax.experimental import pallas as pl
from jax.experimental.pallas import tpu as pltpu
from jax.sharding import PartitionSpec as P

SMALL = 8 * 2**20
WHOLE = 64560 * 2**10


def vmem():
    return pl.BlockSpec(memory_space=pltpu.VMEM)


def hbm():
    return pl.BlockSpec(memory_space=pltpu.HBM)


def folded_hot(cells, depth, lines, fold):
    few = lines // fold
    line = jnp.right_shift(cells, depth.bit_length() - 1)
    own = jnp.bitwise_and(line, few - 1)
    key = jnp.right_shift(line, few.bit_length() - 1) * depth + jnp.bitwise_and(cells, depth - 1)
    at = lax.broadcasted_iota(jnp.int32, (fold * depth, cells.shape[1]), 0)
    return jnp.where(at == key, 1.0, 0.0).astype(jnp.bfloat16), own


def root_first(count):
    root = count * 9 // 16
    return [root] + [index for index in range(count) if index != root]


def far_first(rows, cols):
    share = cols // 4
    return [
        row * cols + quarter * share + col
        for quarter in range(4)[::-1]
        for col in range(share)
        for row in range(rows)
    ]


def by_sender(tiles, rows, cols):
    share = cols // 4
    parts = tiles.reshape((4, share, rows) + tiles.shape[1:])
    blocks = [parts[3 - quarter, :, row] for row in range(rows) for quarter in range(4)]
    return jnp.concatenate(blocks, axis=0)


def tile_shape(slot_len, comps):
    groups = 3 if slot_len % 6 == 0 else 1
    return slot_len // (2 * groups), groups


def trace_kernel(dims, row_swaps, target_hbm, cell_hbm, field_hbm, tile_hbm, *rest):
    comps, width_x, width_y, depth, rows, cols = dims
    row_faces, col_faces = rest[:row_swaps], rest[row_swaps : row_swaps + 2]
    target_ref, cell_ref, field_ref, lhs_ref, tile_ref, side_ref, arrived, left_sem = rest[
        row_swaps + 2 :
    ]
    lines = width_x * width_y
    nodes = cell_ref.shape[1]
    slot_len = nodes // cols
    chunks, few = lhs_ref.shape[:2]
    fold = lines // few
    span = comps // chunks
    copies = [pltpu.make_async_copy(cell_hbm, cell_ref, arrived.at[chunks])]
    for chunk in range(chunks):
        part = pl.ds(chunk * span, span)
        copies.append(
            pltpu.make_async_copy(field_hbm.at[part], field_ref.at[part], arrived.at[chunk])
        )
    copies.append(pltpu.make_async_copy(target_hbm, target_ref, arrived.at[chunks + 1]))
    for copy in copies:
        copy.start()
    sent = []
    copies[0].wait()
    hot, own = folded_hot(cell_ref[...], depth, lines, fold)
    own = jnp.broadcast_to(own, (8, nodes))
    flat = field_ref.reshape(comps * lines, depth)
    found = []
    for chunk in range(chunks):
        copies[1 + chunk].wait()
        for line in range(lines):
            lhs_ref[chunk, line % few, :, pl.ds(line // few * depth, depth)] = flat[
                pl.ds(chunk * span * lines + line, span, stride=lines), :
            ].astype(jnp.bfloat16)
        total = jnp.zeros((span // 8, 8, nodes), jnp.float32)
        group = min(4, few)
        for first in range(0, few, group):
            block = jnp.dot(
                lhs_ref[chunk, first : first + group].reshape(group * span, fold * depth),
                hot,
                preferred_element_type=jnp.float32,
            ).reshape(group, span // 8, 8, nodes)
            for line in range(group):
                total = jnp.where((own == first + line)[None], block[line], total)
        found.append(total.reshape(span, nodes))
    col_odd = lax.rem(lax.axis_index("col"), 2)
    for swap, face_ref in enumerate(col_faces):
        layer = jnp.where(col_odd == swap, width_x - 1, 0)
        start = pl.multiple_of(layer * width_y, width_y)
        sent.append(
            pltpu.make_async_copy(
                field_ref.at[:, pl.ds(start, width_y), :], face_ref, left_sem.at[swap]
            )
        )
        sent[-1].start()
    by_node = jnp.concatenate(found, axis=0).T
    copies[-1].wait()
    tile_rows, groups = tile_shape(slot_len, comps)
    for slot in range(cols):
        pieces = []
        for group in range(2 * groups):
            node = slot * slot_len + group * tile_rows
            pieces.append(by_node[node : node + tile_rows])
        tile = jnp.concatenate(pieces, axis=1).astype(jnp.bfloat16)
        target = target_ref[0, slot]
        share = cols // 4
        quarter = jnp.right_shift(target, share.bit_length() - 1)
        place = ((3 - quarter) * share + jnp.bitwise_and(target, share - 1)) * rows
        for row in range(rows):
            tile_ref[place + row] = tile
    sent.append(pltpu.make_async_copy(tile_ref, tile_hbm, left_sem.at[2 + row_swaps]))
    sent[-1].start()
    row_odd = lax.rem(lax.axis_index("row"), 2)
    for swap, face_ref in enumerate(row_faces):
        low, high = (
            flat[pl.ds(layer, comps * width_x, stride=width_y), :] for layer in (0, width_y - 1)
        )
        side_ref[swap] = jnp.where(row_odd == swap, high, low).astype(jnp.bfloat16)
        sent.append(pltpu.make_async_copy(side_ref.at[swap], face_ref, left_sem.at[2 + swap]))
        sent[-1].start()
    for copy in sent:
        copy.wait()


def corner_kernel(dims, first_ref, second_ref, *out_refs):
    comps, width_x, width_y = dims[:3]
    odd = lax.rem(lax.axis_index("row"), 2)
    for swap, out_ref in enumerate(out_refs):
        for index, ref in enumerate((first_ref, second_ref)):
            low, high = (ref[pl.ds(layer, comps, stride=width_y), :] for layer in (0, width_y - 1))
            line = jnp.where(odd == swap, high, low)
            out_ref[pl.ds(index * comps, comps), :] = (2.0 * line + side_z(line)).astype(
                out_ref.dtype
            )


def unpack_tiles(tiles, comps):
    groups = tiles.shape[2] // comps
    parts = [tiles[:, :, group * comps : (group + 1) * comps] for group in range(groups)]
    return jnp.concatenate(parts, axis=1).reshape(-1, comps)


def boundary_kernel(dims, own_rows, trace_ref, real_ref, imag_ref, row_ref, out_ref):
    if len(trace_ref.shape) == 3:
        tiles = by_sender(trace_ref[...].astype(jnp.float32), *dims[-2:])
        traces = unpack_tiles(tiles, out_ref.shape[2] // 2)
    else:
        traces = trace_ref[...].astype(jnp.float32)
    comps = traces.shape[1]
    angles = comps // 2
    traces = traces.astype(jnp.bfloat16)
    image = jnp.dot(real_ref[...], traces, preferred_element_type=jnp.float32)
    other = jnp.dot(imag_ref[...], traces, preferred_element_type=jnp.float32)
    image = image + jnp.concatenate([-other[:, angles:], other[:, :angles]], axis=1)
    image = image.reshape(image.shape[0] // own_rows, own_rows, comps)
    half = own_rows // 2
    packed = jnp.concatenate([image[:, :half], image[:, half:]], axis=2).astype(out_ref.dtype)
    for place, col in enumerate(root_first(packed.shape[0])):
        out_ref[place] = packed[col]


def shifted_z(values, step):
    rows, depth = values.shape
    at_z = lax.broadcasted_iota(jnp.int32, (rows, depth), 1)
    outside = at_z == (0 if step == 1 else depth - 1)
    return jnp.where(outside, 0.0, pltpu.roll(values, step % depth, 1))


def side_z(values):
    return shifted_z(values, 1) + shifted_z(values, -1)


def volume_kernel(dims, row_swaps, *refs):
    comps, width_x, width_y, depth, rows, cols = dims
    field_ref, medium_ref, flux_ref, cell_ref = refs[:4]
    row_refs = refs[4 : 4 + row_swaps]
    first_ref, second_ref = refs[4 + row_swaps : 6 + row_swaps]
    out_hbm, edge_ref, lhs_ref, taken_ref, out_ref, side_ref, sent = refs[6 + row_swaps :]
    for index, row_ref in enumerate(row_refs):
        side_ref[index] = row_ref[...].astype(jnp.float32)
    lines = width_x * width_y
    nodes = cell_ref.shape[1]
    fold = 2
    few = lines // fold
    hot, own = folded_hot(cell_ref[...], depth, lines, fold)
    at_line = lax.broadcasted_iota(jnp.int32, (few, nodes), 0)
    line_hot = jnp.where(at_line == own, 1.0, 0.0)
    for comp in range(comps):
        lhs_ref[pl.ds(comp * few, few), :] = (
            line_hot * jnp.broadcast_to(flux_ref[comp], (few, nodes))
        ).astype(jnp.bfloat16)
    taken_ref[...] = lax.dot_general(
        lhs_ref[...], hot, (((1,), (1,)), ((), ())), preferred_element_type=jnp.float32
    )

    row_odd = lax.rem(lax.axis_index("row"), 2) == 1
    col_odd = lax.rem(lax.axis_index("col"), 2) == 1
    shape = (width_y, depth)
    at_y = lax.broadcasted_iota(jnp.int32, shape, 0)
    low_y, high_y = at_y == 0, at_y == width_y - 1
    weight = [1.0 / 12.0 + medium_ref[pl.ds(x * width_y, width_y), :] / 27.0 for x in range(width_x)]
    from_first = jnp.logical_or(
        jnp.logical_and(high_y, jnp.logical_not(row_odd)), jnp.logical_and(low_y, row_odd)
    )

    def side_y(values, ends):
        lower = jnp.where(low_y, ends, pltpu.roll(values, 1, 0))
        upper = jnp.where(high_y, ends, pltpu.roll(values, width_y - 1, 0))
        return lower + upper

    def wide(ref, index):
        return jnp.broadcast_to(ref[pl.ds(index, 1), :], shape)

    def component(comp):
        base = comp * lines
        planes = [
            field_ref[pl.ds(base + x * width_y, width_y), :]
            for x in range(width_x)
        ]
        face = pl.ds(comp * width_y, width_y)
        first, second = first_ref[face, :], second_ref[face, :]
        planes = (
            [jnp.where(col_odd, first, second)] + planes + [jnp.where(col_odd, second, first)]
        )
        ends = []
        for x in range(width_x):
            line = [wide(side_ref.at[index], comp * width_x + x) for index in range(row_swaps)]
            ends.append(jnp.where(from_first, line[0], line[1] if row_swaps > 1 else 0.0))
        none = jnp.zeros(shape, jnp.float32)
        ends = [none] + ends + [none]
        for x in range(width_x):
            centre = planes[x + 1]
            sides = planes[x] + planes[x + 2]
            over_x = 2.0 * centre + sides
            ends_x = 2.0 * ends[x + 1] + (ends[x] + ends[x + 2])
            over_xy = 2.0 * over_x + side_y(over_x, ends_x)
            over_xyz = 2.0 * over_xy + side_z(over_xy)
            near = sides + side_y(centre, ends[x + 1]) + side_z(centre)
            here = pl.ds(base + x * width_y, width_y)
            image = (
                (10.0 / 3.0) * centre
                + (1.0 / 3.0) * near
                - weight[x] * over_xyz
                - taken_ref[
                    pl.ds(
                        pl.multiple_of(comp * few + x * width_y % few, width_y), width_y
                    ),
                    pl.ds(x * width_y // few * depth, depth),
                ]
            )
            out_ref[here, :] = image
            for side in range(2):
                if x == side * (width_x - 1):
                    edge_ref[side, face, :] = image

    steps = sent.shape[0]
    together = comps // steps
    copies = []
    for step in range(steps):
        for comp in range(step * together, (step + 1) * together):
            component(comp)
        here = pl.ds(step * together * lines, together * lines)
        copies.append(
            pltpu.make_async_copy(out_ref.at[here, :], out_hbm.at[here, :], sent.at[step])
        )
        copies[-1].start()
    for copy in copies:
        copy.wait()


def last_kernel(
    dims, row_swaps, part_ref, medium_ref, edge_ref, *refs
):
    comps, width_x, width_y, depth, rows, cols = dims
    corner_refs = refs[:row_swaps]
    image_ref, volume_ref, plane_ref, total_ref, sent = refs[row_swaps + 1 :]
    row_odd = lax.rem(lax.axis_index("row"), 2)
    col_odd = lax.rem(lax.axis_index("col"), 2) == 1
    copies = []
    at_row = lax.broadcasted_iota(jnp.int32, (width_y, depth), 0)
    for side in range(2):
        at_x = side * (width_x - 1)
        weight = 1.0 / 12.0 + medium_ref[pl.ds(at_x * width_y, width_y), :] / 27.0
        plane = edge_ref[side].reshape(comps, width_y, depth)
        for index in range(row_swaps):
            first = corner_refs[index][pl.ds(0, comps), :].astype(jnp.float32)
            second = corner_refs[index][pl.ds(comps, comps), :].astype(jnp.float32)
            line = jnp.where(col_odd, second, first) if side else jnp.where(col_odd, first, second)
            at_y = jnp.where(row_odd == index, width_y - 1, 0)
            share = jnp.where(at_row == at_y, weight, 0.0)
            plane = plane - share[None] * line[:, None, :]
        plane_ref[side] = plane.reshape(comps * width_y, depth)
        copies.append(
            pltpu.make_async_copy(
                plane_ref.at[side].reshape(comps, width_y, depth),
                volume_ref.at[:, pl.ds(at_x * width_y, width_y), :],
                sent.at[side],
            )
        )
        copies[-1].start()
    total = jnp.sum(part_ref[...].astype(jnp.float32), axis=0)
    half, lanes = total.shape
    total_ref[:half] = total[:, : lanes // 2]
    total_ref[half:] = total[:, lanes // 2 :]
    copies.append(pltpu.make_async_copy(total_ref, image_ref, sent.at[2]))
    copies[-1].start()
    for copy in copies:
        copy.wait()


def swap_pairs(count, swap):
    pairs = []
    for low in range(swap, count - 1, 2):
        pairs += [(low, low + 1), (low + 1, low)]
    return pairs


def on_device(wave_field, medium_term, node_flux, node_cell, block_target, boundary_matrix):
    comps, width_x, width_y, depth = wave_field.shape
    rows, cols = lax.axis_size("row"), lax.axis_size("col")
    dims = (comps, width_x, width_y, depth, rows, cols)
    lines = width_x * width_y
    nodes = node_cell.shape[-1]
    slot_len = nodes // cols
    row_swaps = 1 if rows == 2 else 2
    slab_rows, span = boundary_matrix.shape[1:]
    own_rows = slab_rows // cols
    f32, bf16 = jnp.float32, jnp.bfloat16
    params = pltpu.CompilerParams(vmem_limit_bytes=SMALL)

    chunks, fold = 2, 4
    tile_rows, groups = tile_shape(slot_len, comps)
    tile_dims = (tile_rows, 2 * groups * comps)
    field = wave_field.reshape(comps * lines, depth)
    cells = node_cell.reshape(1, nodes)
    targets = block_target.reshape(1, cols)
    flux = node_flux.reshape(comps, 1, nodes)
    medium = medium_term.reshape(lines, depth)

    tiles, *faces = pl.pallas_call(
        functools.partial(trace_kernel, dims, row_swaps),
        out_shape=[jax.ShapeDtypeStruct((rows * cols,) + tile_dims, bf16)]
        + [jax.ShapeDtypeStruct((comps * width_x, depth), bf16)] * row_swaps
        + [jax.ShapeDtypeStruct((comps, width_y, depth), f32)] * 2,
        in_specs=[hbm()] * 3,
        out_specs=[hbm()] * (3 + row_swaps),
        scratch_shapes=[
            pltpu.SMEM((1, cols), jnp.int32),
            pltpu.VMEM((1, nodes), jnp.int32),
            pltpu.VMEM((comps, lines, depth), f32),
            pltpu.VMEM((chunks, lines // fold, comps // chunks, fold * depth), bf16),
            pltpu.VMEM((rows * cols,) + tile_dims, bf16),
            pltpu.VMEM((row_swaps, comps * width_x, depth), bf16),
            pltpu.SemaphoreType.DMA((chunks + 2,)),
            pltpu.SemaphoreType.DMA((3 + row_swaps,)),
        ],
        compiler_params=pltpu.CompilerParams(vmem_limit_bytes=WHOLE),
        name="traces",
    )(targets, cells, field.reshape(comps, lines, depth))
    col_sides = [
        lax.ppermute(face, "col", swap_pairs(cols, swap)).reshape(comps * width_y, depth)
        for swap, face in enumerate(faces[row_swaps : row_swaps + 2])
    ]
    row_sides = [
        lax.ppermute(face, "row", swap_pairs(rows, swap))
        for swap, face in enumerate(faces[:row_swaps])
    ]
    received = lax.all_to_all(
        tiles, ("row", "col"), 0, 0, tiled=True, axis_index_groups=[far_first(rows, cols)]
    )

    if slot_len % 8:
        received = unpack_tiles(by_sender(received, rows, cols), comps)
    shares = pl.pallas_call(
        functools.partial(boundary_kernel, dims, own_rows),
        out_shape=jax.ShapeDtypeStruct((cols, own_rows // 2, 2 * comps), bf16),
        in_specs=[vmem()] * 4,
        out_specs=vmem(),
        compiler_params=params,
        name="boundary",
    )(received, boundary_matrix[0], boundary_matrix[1], row_sides[0])
    shares = lax.all_to_all(
        shares, "col", 0, 0, tiled=True, axis_index_groups=[root_first(cols)]
    )

    corners = pl.pallas_call(
        functools.partial(corner_kernel, dims),
        out_shape=[jax.ShapeDtypeStruct((2 * comps, depth), bf16)] * row_swaps,
        in_specs=[vmem()] * 2,
        out_specs=[vmem()] * row_swaps,
        compiler_params=params,
        name="corners",
    )(*col_sides)
    corner_sides = [
        lax.ppermute(lines_of, "row", swap_pairs(rows, swap))
        for swap, lines_of in enumerate(corners)
    ]

    volume, edges = pl.pallas_call(
        functools.partial(volume_kernel, dims, row_swaps),
        out_shape=[
            jax.ShapeDtypeStruct((comps * lines, depth), f32),
            jax.ShapeDtypeStruct((2, comps * width_y, depth), f32),
        ],
        in_specs=[vmem()] * (6 + row_swaps),
        out_specs=[hbm(), vmem()],
        scratch_shapes=[
            pltpu.VMEM((comps * lines // 2, nodes), bf16),
            pltpu.VMEM((comps * lines // 2, 2 * depth), f32),
            pltpu.VMEM((comps * lines, depth), f32),
            pltpu.VMEM((row_swaps, comps * width_x, depth), f32),
            pltpu.SemaphoreType.DMA((8,)),
        ],
        compiler_params=params,
        name="volume",
    )(field, medium, flux, cells, *row_sides, *col_sides)

    boundary_image, volume = pl.pallas_call(
        functools.partial(last_kernel, dims, row_swaps),
        out_shape=[
            jax.ShapeDtypeStruct((own_rows, comps), f32),
            jax.ShapeDtypeStruct((comps, lines, depth), f32),
        ],
        in_specs=[vmem()] * (3 + row_swaps) + [hbm()],
        out_specs=[hbm(), hbm()],
        scratch_shapes=[
            pltpu.VMEM((2, comps * width_y, depth), f32),
            pltpu.VMEM((own_rows, comps), f32),
            pltpu.SemaphoreType.DMA((3,)),
        ],
        input_output_aliases={3 + row_swaps: 1},
        compiler_params=params,
        name="last",
    )(shares, medium, edges, *corner_sides, volume.reshape(comps, lines, depth))
    return (volume.reshape(comps, width_x, width_y, depth), boundary_image)


def solution(mesh):
    in_specs = (
        P(None, "col", "row", None),
        P("col", "row", None),
        P(None, "col", "row", None),
        P("col", "row", None),
        P("col", "row", None),
        P(None, "row", "col"),
    )
    out_specs = (P(None, "col", "row", None), P(("row", "col"), None))
    return jax.shard_map(
        on_device, mesh=mesh, in_specs=in_specs, out_specs=out_specs, check_vma=False
    )
```

```python
import functools

import jax
import jax.numpy as jnp
from jax import lax
from jax.experimental import pallas as pl
from jax.experimental.pallas import tpu as pltpu
from jax.sharding import PartitionSpec as P

TILE_ROWS = 16
SMALL = 8 * 2**20
WHOLE = 64560 * 2**10


def vmem():
    return pl.BlockSpec(memory_space=pltpu.VMEM)


def hbm():
    return pl.BlockSpec(memory_space=pltpu.HBM)


def folded_hot(cells, depth, lines, fold):
    few = lines // fold
    line = jnp.right_shift(cells, depth.bit_length() - 1)
    own = jnp.bitwise_and(line, few - 1)
    key = jnp.right_shift(line, few.bit_length() - 1) * depth + jnp.bitwise_and(cells, depth - 1)
    at = lax.broadcasted_iota(jnp.int32, (fold * depth, cells.shape[1]), 0)
    return jnp.where(at == key, 1.0, 0.0).astype(jnp.bfloat16), own


def root_first(count):
    root = count * 9 // 16
    return [root] + [index for index in range(count) if index != root]


def trace_kernel(dims, row_swaps, target_hbm, cell_hbm, field_hbm, tile_hbm, *rest):
    comps, width_x, width_y, depth, rows, cols = dims
    row_faces, col_faces = rest[:row_swaps], rest[row_swaps : row_swaps + 2]
    target_ref, cell_ref, field_ref, lhs_ref, tile_ref, side_ref, arrived, left_sem = rest[
        row_swaps + 2 :
    ]
    lines = width_x * width_y
    nodes = cell_ref.shape[1]
    slot_len = nodes // cols
    chunks, few = lhs_ref.shape[:2]
    fold = lines // few
    span = comps // chunks
    copies = [pltpu.make_async_copy(cell_hbm, cell_ref, arrived.at[chunks])]
    for chunk in range(chunks):
        part = pl.ds(chunk * span, span)
        copies.append(
            pltpu.make_async_copy(field_hbm.at[part], field_ref.at[part], arrived.at[chunk])
        )
    copies.append(pltpu.make_async_copy(target_hbm, target_ref, arrived.at[chunks + 1]))
    for copy in copies:
        copy.start()
    sent = []
    copies[0].wait()
    hot, own = folded_hot(cell_ref[...], depth, lines, fold)
    own = jnp.broadcast_to(own, (8, nodes))
    flat = field_ref.reshape(comps * lines, depth)
    found = []
    for chunk in range(chunks):
        copies[1 + chunk].wait()
        for line in range(lines):
            lhs_ref[chunk, line % few, :, pl.ds(line // few * depth, depth)] = flat[
                pl.ds(chunk * span * lines + line, span, stride=lines), :
            ].astype(jnp.bfloat16)
        total = jnp.zeros((span // 8, 8, nodes), jnp.float32)
        group = min(4, few)
        for first in range(0, few, group):
            block = jnp.dot(
                lhs_ref[chunk, first : first + group].reshape(group * span, fold * depth),
                hot,
                preferred_element_type=jnp.float32,
            ).reshape(group, span // 8, 8, nodes)
            for line in range(group):
                total = jnp.where((own == first + line)[None], block[line], total)
        found.append(total.reshape(span, nodes))
    col_odd = lax.rem(lax.axis_index("col"), 2)
    for swap, face_ref in enumerate(col_faces):
        layer = jnp.where(col_odd == swap, width_x - 1, 0)
        start = pl.multiple_of(layer * width_y, width_y)
        sent.append(
            pltpu.make_async_copy(
                field_ref.at[:, pl.ds(start, width_y), :], face_ref, left_sem.at[swap]
            )
        )
        sent[-1].start()
    by_node = jnp.concatenate(found, axis=0).T
    copies[-1].wait()
    left_len = min(slot_len, TILE_ROWS)
    for slot in range(cols):
        piece = by_node[slot * slot_len : (slot + 1) * slot_len]
        left = piece[:left_len]
        right = piece[left_len:]
        if left_len < TILE_ROWS:
            left = jnp.concatenate(
                [left, jnp.zeros((TILE_ROWS - left_len, comps), jnp.float32)], axis=0
            )
        gap = TILE_ROWS - (slot_len - left_len)
        if slot_len == left_len:
            right = jnp.zeros((TILE_ROWS, comps), jnp.float32)
        elif gap:
            right = jnp.concatenate([right, jnp.zeros((gap, comps), jnp.float32)], axis=0)
        tile = jnp.concatenate([left, right], axis=1).astype(jnp.bfloat16)
        for row in range(rows):
            tile_ref[row * cols + target_ref[0, slot]] = tile
    sent.append(pltpu.make_async_copy(tile_ref, tile_hbm, left_sem.at[2 + row_swaps]))
    sent[-1].start()
    row_odd = lax.rem(lax.axis_index("row"), 2)
    for swap, face_ref in enumerate(row_faces):
        low, high = (
            flat[pl.ds(layer, comps * width_x, stride=width_y), :] for layer in (0, width_y - 1)
        )
        side_ref[swap] = jnp.where(row_odd == swap, high, low).astype(jnp.bfloat16)
        sent.append(pltpu.make_async_copy(side_ref.at[swap], face_ref, left_sem.at[2 + swap]))
        sent[-1].start()
    for copy in sent:
        copy.wait()


def corner_kernel(dims, first_ref, second_ref, *out_refs):
    comps, width_x, width_y = dims[:3]
    odd = lax.rem(lax.axis_index("row"), 2)
    for swap, out_ref in enumerate(out_refs):
        for index, ref in enumerate((first_ref, second_ref)):
            low, high = (ref[pl.ds(layer, comps, stride=width_y), :] for layer in (0, width_y - 1))
            line = jnp.where(odd == swap, high, low)
            out_ref[pl.ds(index * comps, comps), :] = (2.0 * line + side_z(line)).astype(
                out_ref.dtype
            )


def unpack_tiles(tiles, slot_len, comps):
    left_len = min(slot_len, TILE_ROWS)
    parts = [tiles[:, :left_len, :comps]]
    if slot_len > left_len:
        parts.append(tiles[:, : slot_len - left_len, comps:])
    both = jnp.concatenate(parts, axis=1) if len(parts) > 1 else parts[0]
    return both.reshape(tiles.shape[0] * slot_len, comps)


def boundary_kernel(slot_len, own_rows, trace_ref, real_ref, imag_ref, row_ref, out_ref):
    if len(trace_ref.shape) == 3:
        traces = unpack_tiles(
            trace_ref[...].astype(jnp.float32), slot_len, trace_ref.shape[2] // 2
        )
    else:
        traces = trace_ref[...].astype(jnp.float32)
    comps = traces.shape[1]
    angles = comps // 2
    traces = traces.astype(jnp.bfloat16)
    image = jnp.dot(real_ref[...], traces, preferred_element_type=jnp.float32)
    other = jnp.dot(imag_ref[...], traces, preferred_element_type=jnp.float32)
    image = image + jnp.concatenate([-other[:, angles:], other[:, :angles]], axis=1)
    image = image.reshape(image.shape[0] // own_rows, own_rows, comps)
    half = own_rows // 2
    packed = jnp.concatenate([image[:, :half], image[:, half:]], axis=2).astype(out_ref.dtype)
    for place, col in enumerate(root_first(packed.shape[0])):
        out_ref[place] = packed[col]


def shifted_z(values, step):
    rows, depth = values.shape
    at_z = lax.broadcasted_iota(jnp.int32, (rows, depth), 1)
    outside = at_z == (0 if step == 1 else depth - 1)
    return jnp.where(outside, 0.0, pltpu.roll(values, step % depth, 1))


def side_z(values):
    return shifted_z(values, 1) + shifted_z(values, -1)


def volume_kernel(dims, row_swaps, *refs):
    comps, width_x, width_y, depth, rows, cols = dims
    field_ref, medium_ref, flux_ref, cell_ref = refs[:4]
    row_refs = refs[4 : 4 + row_swaps]
    first_ref, second_ref = refs[4 + row_swaps : 6 + row_swaps]
    out_hbm, edge_ref, lhs_ref, taken_ref, out_ref, side_ref, sent = refs[6 + row_swaps :]
    for index, row_ref in enumerate(row_refs):
        side_ref[index] = row_ref[...].astype(jnp.float32)
    lines = width_x * width_y
    nodes = cell_ref.shape[1]
    fold = 2
    few = lines // fold
    hot, own = folded_hot(cell_ref[...], depth, lines, fold)
    at_line = lax.broadcasted_iota(jnp.int32, (few, nodes), 0)
    line_hot = jnp.where(at_line == own, 1.0, 0.0)
    for comp in range(comps):
        lhs_ref[pl.ds(comp * few, few), :] = (
            line_hot * jnp.broadcast_to(flux_ref[comp], (few, nodes))
        ).astype(jnp.bfloat16)
    taken_ref[...] = lax.dot_general(
        lhs_ref[...], hot, (((1,), (1,)), ((), ())), preferred_element_type=jnp.float32
    )

    row_odd = lax.rem(lax.axis_index("row"), 2) == 1
    col_odd = lax.rem(lax.axis_index("col"), 2) == 1
    shape = (width_y, depth)
    at_y = lax.broadcasted_iota(jnp.int32, shape, 0)
    low_y, high_y = at_y == 0, at_y == width_y - 1
    weight = [1.0 / 12.0 + medium_ref[pl.ds(x * width_y, width_y), :] / 27.0 for x in range(width_x)]
    from_first = jnp.logical_or(
        jnp.logical_and(high_y, jnp.logical_not(row_odd)), jnp.logical_and(low_y, row_odd)
    )

    def side_y(values, ends):
        lower = jnp.where(low_y, ends, pltpu.roll(values, 1, 0))
        upper = jnp.where(high_y, ends, pltpu.roll(values, width_y - 1, 0))
        return lower + upper

    def wide(ref, index):
        return jnp.broadcast_to(ref[pl.ds(index, 1), :], shape)

    def component(comp):
        base = comp * lines
        planes = [
            field_ref[pl.ds(base + x * width_y, width_y), :]
            for x in range(width_x)
        ]
        face = pl.ds(comp * width_y, width_y)
        first, second = first_ref[face, :], second_ref[face, :]
        planes = (
            [jnp.where(col_odd, first, second)] + planes + [jnp.where(col_odd, second, first)]
        )
        ends = []
        for x in range(width_x):
            line = [wide(side_ref.at[index], comp * width_x + x) for index in range(row_swaps)]
            ends.append(jnp.where(from_first, line[0], line[1] if row_swaps > 1 else 0.0))
        none = jnp.zeros(shape, jnp.float32)
        ends = [none] + ends + [none]
        for x in range(width_x):
            centre = planes[x + 1]
            sides = planes[x] + planes[x + 2]
            over_x = 2.0 * centre + sides
            ends_x = 2.0 * ends[x + 1] + (ends[x] + ends[x + 2])
            over_xy = 2.0 * over_x + side_y(over_x, ends_x)
            over_xyz = 2.0 * over_xy + side_z(over_xy)
            near = sides + side_y(centre, ends[x + 1]) + side_z(centre)
            here = pl.ds(base + x * width_y, width_y)
            image = (
                (10.0 / 3.0) * centre
                + (1.0 / 3.0) * near
                - weight[x] * over_xyz
                - taken_ref[
                    pl.ds(
                        pl.multiple_of(comp * few + x * width_y % few, width_y), width_y
                    ),
                    pl.ds(x * width_y // few * depth, depth),
                ]
            )
            out_ref[here, :] = image
            for side in range(2):
                if x == side * (width_x - 1):
                    edge_ref[side, face, :] = image

    steps = sent.shape[0]
    together = comps // steps
    copies = []
    for step in range(steps):
        for comp in range(step * together, (step + 1) * together):
            component(comp)
        here = pl.ds(step * together * lines, together * lines)
        copies.append(
            pltpu.make_async_copy(out_ref.at[here, :], out_hbm.at[here, :], sent.at[step])
        )
        copies[-1].start()
    for copy in copies:
        copy.wait()


def last_kernel(
    dims, row_swaps, part_ref, medium_ref, edge_ref, *refs
):
    comps, width_x, width_y, depth, rows, cols = dims
    corner_refs = refs[:row_swaps]
    image_ref, volume_ref, plane_ref, total_ref, sent = refs[row_swaps + 1 :]
    row_odd = lax.rem(lax.axis_index("row"), 2)
    col_odd = lax.rem(lax.axis_index("col"), 2) == 1
    copies = []
    at_row = lax.broadcasted_iota(jnp.int32, (width_y, depth), 0)
    for side in range(2):
        at_x = side * (width_x - 1)
        weight = 1.0 / 12.0 + medium_ref[pl.ds(at_x * width_y, width_y), :] / 27.0
        plane = edge_ref[side].reshape(comps, width_y, depth)
        for index in range(row_swaps):
            first = corner_refs[index][pl.ds(0, comps), :].astype(jnp.float32)
            second = corner_refs[index][pl.ds(comps, comps), :].astype(jnp.float32)
            line = jnp.where(col_odd, second, first) if side else jnp.where(col_odd, first, second)
            at_y = jnp.where(row_odd == index, width_y - 1, 0)
            share = jnp.where(at_row == at_y, weight, 0.0)
            plane = plane - share[None] * line[:, None, :]
        plane_ref[side] = plane.reshape(comps * width_y, depth)
        copies.append(
            pltpu.make_async_copy(
                plane_ref.at[side].reshape(comps, width_y, depth),
                volume_ref.at[:, pl.ds(at_x * width_y, width_y), :],
                sent.at[side],
            )
        )
        copies[-1].start()
    total = jnp.sum(part_ref[...].astype(jnp.float32), axis=0)
    half, lanes = total.shape
    total_ref[:half] = total[:, : lanes // 2]
    total_ref[half:] = total[:, lanes // 2 :]
    copies.append(pltpu.make_async_copy(total_ref, image_ref, sent.at[2]))
    copies[-1].start()
    for copy in copies:
        copy.wait()


def swap_pairs(count, swap):
    pairs = []
    for low in range(swap, count - 1, 2):
        pairs += [(low, low + 1), (low + 1, low)]
    return pairs


def on_device(wave_field, medium_term, node_flux, node_cell, block_target, boundary_matrix):
    comps, width_x, width_y, depth = wave_field.shape
    rows, cols = lax.axis_size("row"), lax.axis_size("col")
    dims = (comps, width_x, width_y, depth, rows, cols)
    lines = width_x * width_y
    nodes = node_cell.shape[-1]
    slot_len = nodes // cols
    row_swaps = 1 if rows == 2 else 2
    slab_rows, span = boundary_matrix.shape[1:]
    own_rows = slab_rows // cols
    f32, bf16 = jnp.float32, jnp.bfloat16
    params = pltpu.CompilerParams(vmem_limit_bytes=SMALL)

    chunks, fold = 2, 4
    field = wave_field.reshape(comps * lines, depth)
    cells = node_cell.reshape(1, nodes)
    targets = block_target.reshape(1, cols)
    flux = node_flux.reshape(comps, 1, nodes)
    medium = medium_term.reshape(lines, depth)

    tiles, *faces = pl.pallas_call(
        functools.partial(trace_kernel, dims, row_swaps),
        out_shape=[jax.ShapeDtypeStruct((rows * cols, TILE_ROWS, 2 * comps), bf16)]
        + [jax.ShapeDtypeStruct((comps * width_x, depth), bf16)] * row_swaps
        + [jax.ShapeDtypeStruct((comps, width_y, depth), f32)] * 2,
        in_specs=[hbm()] * 3,
        out_specs=[hbm()] * (3 + row_swaps),
        scratch_shapes=[
            pltpu.SMEM((1, cols), jnp.int32),
            pltpu.VMEM((1, nodes), jnp.int32),
            pltpu.VMEM((comps, lines, depth), f32),
            pltpu.VMEM((chunks, lines // fold, comps // chunks, fold * depth), bf16),
            pltpu.VMEM((rows * cols, TILE_ROWS, 2 * comps), bf16),
            pltpu.VMEM((row_swaps, comps * width_x, depth), bf16),
            pltpu.SemaphoreType.DMA((chunks + 2,)),
            pltpu.SemaphoreType.DMA((3 + row_swaps,)),
        ],
        compiler_params=pltpu.CompilerParams(vmem_limit_bytes=WHOLE),
        name="traces",
    )(targets, cells, field.reshape(comps, lines, depth))
    col_sides = [
        lax.ppermute(face, "col", swap_pairs(cols, swap)).reshape(comps * width_y, depth)
        for swap, face in enumerate(faces[row_swaps : row_swaps + 2])
    ]
    row_sides = [
        lax.ppermute(face, "row", swap_pairs(rows, swap))
        for swap, face in enumerate(faces[:row_swaps])
    ]
    received = lax.all_to_all(tiles, ("row", "col"), 0, 0, tiled=True)

    if slot_len % 8:
        received = unpack_tiles(received, slot_len, comps)
    shares = pl.pallas_call(
        functools.partial(boundary_kernel, slot_len, own_rows),
        out_shape=jax.ShapeDtypeStruct((cols, own_rows // 2, 2 * comps), bf16),
        in_specs=[vmem()] * 4,
        out_specs=vmem(),
        compiler_params=params,
        name="boundary",
    )(received, boundary_matrix[0], boundary_matrix[1], row_sides[0])
    shares = lax.all_to_all(
        shares, "col", 0, 0, tiled=True, axis_index_groups=[root_first(cols)]
    )

    corners = pl.pallas_call(
        functools.partial(corner_kernel, dims),
        out_shape=[jax.ShapeDtypeStruct((2 * comps, depth), bf16)] * row_swaps,
        in_specs=[vmem()] * 2,
        out_specs=[vmem()] * row_swaps,
        compiler_params=params,
        name="corners",
    )(*col_sides)
    corner_sides = [
        lax.ppermute(lines_of, "row", swap_pairs(rows, swap))
        for swap, lines_of in enumerate(corners)
    ]

    volume, edges = pl.pallas_call(
        functools.partial(volume_kernel, dims, row_swaps),
        out_shape=[
            jax.ShapeDtypeStruct((comps * lines, depth), f32),
            jax.ShapeDtypeStruct((2, comps * width_y, depth), f32),
        ],
        in_specs=[vmem()] * (6 + row_swaps),
        out_specs=[hbm(), vmem()],
        scratch_shapes=[
            pltpu.VMEM((comps * lines // 2, nodes), bf16),
            pltpu.VMEM((comps * lines // 2, 2 * depth), f32),
            pltpu.VMEM((comps * lines, depth), f32),
            pltpu.VMEM((row_swaps, comps * width_x, depth), f32),
            pltpu.SemaphoreType.DMA((16,)),
        ],
        compiler_params=params,
        name="volume",
    )(field, medium, flux, cells, *row_sides, *col_sides)

    boundary_image, volume = pl.pallas_call(
        functools.partial(last_kernel, dims, row_swaps),
        out_shape=[
            jax.ShapeDtypeStruct((own_rows, comps), f32),
            jax.ShapeDtypeStruct((comps, lines, depth), f32),
        ],
        in_specs=[vmem()] * (3 + row_swaps) + [hbm()],
        out_specs=[hbm(), hbm()],
        scratch_shapes=[
            pltpu.VMEM((2, comps * width_y, depth), f32),
            pltpu.VMEM((own_rows, comps), f32),
            pltpu.SemaphoreType.DMA((3,)),
        ],
        input_output_aliases={3 + row_swaps: 1},
        compiler_params=params,
        name="last",
    )(shares, medium, edges, *corner_sides, volume.reshape(comps, lines, depth))
    return (volume.reshape(comps, width_x, width_y, depth), boundary_image)


def solution(mesh):
    in_specs = (
        P(None, "col", "row", None),
        P("col", "row", None),
        P(None, "col", "row", None),
        P("col", "row", None),
        P("col", "row", None),
        P(None, "row", "col"),
    )
    out_specs = (P(None, "col", "row", None), P(("row", "col"), None))
    return jax.shard_map(
        on_device, mesh=mesh, in_specs=in_specs, out_specs=out_specs, check_vma=False
    )
```
